256 devices in a mesh: leaf: 64 (over y, z, core), col: 4 (over x).
Axes of the slice: x: 4, y: 4, z: 8, core: 2. Of those that a mesh axis runs over, the one named last changes fastest.
Arguments:
- ratings: float32 [65536, 2048], P('leaf', 'col'), may hold values from -6 to 6
- dense_blocks: float32 [64, 1024, 1024], P('leaf'), may hold values from -0.1875 to 0.1875
- row_basis: float32 [64, 1024, 256], P('leaf'), may hold values from -0.375 to 0.375
- col_basis: float32 [64, 1024, 256], P('leaf'), may hold values from -0.1875 to 0.1875
- transfers: float32 [2, 4, 256, 256], replicated, may hold values from -0.1875 to 0.1875
- couplings: float32 [3, 3, 256, 256], replicated, may hold values from -0.21875 to 0.21875
Outputs:
- predicted: float32 [65536, 2048], P('leaf', 'col')
The draws below stay inside these ranges and needn't reach their ends.
All inputs are finite; a program needn't handle non-finite values.
Results may differ from the reference program's by a relative error of at most 0.0001.
Values sent between devices are 32-bit elements; how exact they have to be, the bound alone decides.
No kernel may reach another device: no remote copies, remote signals or barrier semaphores. Data moves between devices by JAX's collectives and lax.ppermute only.
A program may use at most 128 MiB of HBM per device.

```python
import jax
import jax.numpy as jnp
from jax import lax

LEAF = 1024
RANK = 256
COLS = 2048
LEAVES = 64
USERS = 65536
LEVELS = 3
TOPS = 4


def steps_of(rng, extent, cuts, smallest, high):
    loudness, own = 1.0, jax.random.fold_in(rng, 6)
    for axis_at, parts in cuts:
        heights = jnp.exp(jax.random.uniform(jax.random.fold_in(own, axis_at), (parts,), jnp.float32, smallest / len(cuts), high / len(cuts)))
        loudness = loudness * jnp.repeat(heights, extent[axis_at] // parts).reshape([-1 if axis == axis_at else 1 for axis in range(len(extent))])
    return loudness


def noise(own_key, dims, spread, most, pieces=(), dtype=jnp.bfloat16):
    result = spread * jax.random.normal(own_key, dims, jnp.float32)
    if pieces:
        result = result * steps_of(own_key, dims, pieces, -0.22, 0.18)
    return jnp.clip(result, -most, most).astype(dtype)


def setup_inputs(seed: int = 0) -> dict:
    key_of = jax.random.split(jax.random.key(seed), 7)
    ratings = noise(key_of[0], (USERS, COLS), 1.0, 6.0, ((0, 64), (1, 4)), jnp.float32)
    dense_blocks = noise(key_of[1], (LEAVES, LEAF, LEAF), LEAF ** -0.5, 0.1875, ((0, 64),), jnp.float32)
    row_basis = noise(key_of[2], (LEAVES, LEAF, RANK), RANK ** -0.5, 0.375, ((0, 64),), jnp.float32)
    col_basis = noise(key_of[3], (LEAVES, LEAF, RANK), LEAF ** -0.5, 0.1875, ((0, 64),), jnp.float32)
    transfers = noise(key_of[4], (LEVELS - 1, 4, RANK, RANK), (4 * RANK) ** -0.5, 0.1875, (), jnp.float32)
    couplings = noise(key_of[5], (LEVELS, 3, RANK, RANK), (3 * RANK) ** -0.5, 0.21875, (), jnp.float32)
    return dict(ratings=ratings, dense_blocks=dense_blocks, row_basis=row_basis, col_basis=col_basis, transfers=transfers, couplings=couplings)


def reference(ratings, dense_blocks, row_basis, col_basis, transfers, couplings):
    highest = lax.Precision.HIGHEST
    leaves = dense_blocks.shape[0]
    columns = ratings.shape[1]
    per_leaf = ratings.reshape(leaves, LEAF, columns)
    near_part = jnp.einsum("nij,njc->nic", dense_blocks, per_leaf, precision=highest)
    coef = jnp.einsum("nia,nic->nac", col_basis, per_leaf, precision=highest)
    fields = []
    for height in range(LEVELS):
        fanout = 4 if height < LEVELS - 1 else TOPS
        grouped = coef.reshape(-1, fanout, RANK, columns)
        field = jnp.zeros_like(grouped)
        for offset in range(1, fanout):
            rolled = jnp.roll(grouped, -offset, axis=1)
            field = field + jnp.einsum("ab,gibc->giac", couplings[height, offset - 1], rolled, precision=highest)
        fields.append(field)
        if height < LEVELS - 1:
            coef = jnp.einsum("kab,gkac->gbc", transfers[height], grouped, precision=highest)
    downward = fields[-1].reshape(-1, RANK, columns)
    for height in range(LEVELS - 2, -1, -1):
        downward = fields[height] + jnp.einsum("kab,gbc->gkac", transfers[height], downward, precision=highest)
        downward = downward.reshape(-1, RANK, columns)
    far_part = jnp.einsum("nia,nac->nic", row_basis, downward, precision=highest)
    return (near_part + far_part).reshape(ratings.shape)
```

```python
import functools

import jax
import jax.numpy as jnp
from jax import lax
from jax.experimental import pallas as pl
from jax.experimental.pallas import tpu as pltpu
from jax.sharding import PartitionSpec as P

F32 = jnp.float32
HIGH = lax.Precision.HIGH
MIB = 1 << 20


def dot(a, b, ca, cb):
    return lax.dot_general(
        a, b, (((ca,), (cb,)), ((), ())), precision=HIGH, preferred_element_type=F32
    )


def run(body, ins, outs, name, flops, scratch=(), vmem=24):
    ins = [pltpu.with_memory_space_constraint(x, pltpu.VMEM) for x in ins]
    whole = pl.BlockSpec(memory_space=pltpu.VMEM)
    return pl.pallas_call(
        body,
        out_shape=[pltpu.VMEM(shape, F32) for shape in outs],
        in_specs=[whole] * len(ins),
        out_specs=[whole] * len(outs),
        scratch_shapes=list(scratch),
        compiler_params=pltpu.CompilerParams(vmem_limit_bytes=vmem * MIB),
        cost_estimate=pl.CostEstimate(
            flops=flops,
            bytes_accessed=4 * sum(x.size for x in ins),
            transcendentals=0,
        ),
        name=name,
    )(*ins)


def place():
    leaf = lax.axis_index("leaf")
    return leaf % 4, (leaf // 4) % 4, leaf // 16


def other(index, j):
    low, high = index % 2, index // 2
    low = 1 - low if j & 1 else low
    high = 1 - high if j & 2 else high
    return 2 * high + low


def rows(index, count):
    return pl.ds(pl.multiple_of(index * count, count), count)


def leaf_coefficients(x, basis, o0, o1, o2, o3, whole):
    p, _, _ = place()
    whole[...] = dot(x[...], basis[...], 0, 0)
    step = o0.shape[0]
    for j, out in enumerate((o0, o1, o2, o3)):
        out[...] = whole[rows(other(p, j), step), :]


def near_field(dense, x, out):
    @pl.loop(0, 4)
    def _(i):
        at = rows(i, 256)
        out[at, :] = dot(dense[at, :], x[...], 1, 0)


def up(digit, level, c0, c1, c2, c3, transfers, o0, o1, o2, o3, whole):
    own = place()[digit]
    total = None
    for j, c in enumerate((c0, c1, c2, c3)):
        term = dot(c[...], transfers[level, other(own, j)], 1, 0)
        total = term if total is None else total + term
    if o1 is None:
        o0[...] = total
        return
    whole[...] = total
    step = o0.shape[0]
    for j, out in enumerate((o0, o1, o2, o3)):
        out[...] = whole[rows(other(place()[digit + 1], j), step), :]


def up_split(digit, level, c0, c1, c2, c3, transfers, o0, o1, o2, o3, whole):
    up(digit, level, c0, c1, c2, c3, transfers, o0, o1, o2, o3, whole)


def up_last(digit, level, c0, c1, c2, c3, transfers, o0):
    up(digit, level, c0, c1, c2, c3, transfers, o0, None, None, None, None)


def field_of(target, own, parts, level, couplings):
    at = other(own, target)
    total = None
    for j, c in enumerate(parts):
        if j == target:
            continue
        offset = (other(own, j) - at + 4) % 4
        term = dot(c[...], couplings[level, offset - 1], 1, 1)
        total = term if total is None else total + term
    return total


def couple_all(digit, level, c0, c1, c2, c3, couplings, f0, f1, f2, f3):
    own = place()[digit]
    for target, out in enumerate((f0, f1, f2, f3)):
        out[...] = field_of(target, own, (c0, c1, c2, c3), level, couplings)


def top(c0, c1, c2, c3, couplings, transfers, f0, f1, f2, f3, o0, o1, o2, o3):
    _, q, r = place()
    g = field_of(0, r, (c0, c1, c2, c3), 2, couplings)
    for j, (field, out) in enumerate(zip((f0, f1, f2, f3), (o0, o1, o2, o3))):
        out[...] = field[...] + dot(g, transfers[1, other(q, j)], 1, 1)


def down(g0, g1, g2, g3, transfers, f0, f1, f2, f3, o0, o1, o2, o3, whole):
    p, q, _ = place()
    step = g0.shape[0]
    for j, g in enumerate((g0, g1, g2, g3)):
        whole[rows(other(q, j), step), :] = g[...]
    g = whole[...]
    for j, (field, out) in enumerate(zip((f0, f1, f2, f3), (o0, o1, o2, o3))):
        out[...] = field[...] + dot(g, transfers[0, other(p, j)], 1, 1)


def finish(near, row_basis, g0, g1, g2, g3, out, whole):
    @pl.when(pl.program_id(0) == 0)
    def _():
        p, _, _ = place()
        step = g0.shape[0]
        for j, g in enumerate((g0, g1, g2, g3)):
            whole[rows(other(p, j), step), :] = g[...]

    at = rows(pl.program_id(0), out.shape[0])
    out[...] = near[at, :] + dot(row_basis[at, :], whole[...], 1, 1)


def swap(block, bits):
    count = lax.axis_size("leaf")
    return lax.ppermute(block, "leaf", [(i, i ^ bits) for i in range(count)])


def exchange(blocks, digit):
    got = {j: swap(blocks[j], j << 2 * digit) for j in (2, 3, 1)}
    return [blocks[0]] + [got[j] for j in (1, 2, 3)]


def local(ratings, dense_blocks, row_basis, col_basis, transfers, couplings):
    users, columns = ratings.shape
    rank = col_basis.shape[2]
    quarter, slim = columns // 4, columns // 16
    unit = 2 * 3 * rank * rank
    dense, rbasis, cbasis = dense_blocks[0], row_basis[0], col_basis[0]

    coef = run(
        leaf_coefficients,
        [ratings, cbasis],
        [(quarter, rank)] * 4,
        "leaf_coefficients",
        6 * users * columns * rank,
        [pltpu.VMEM((columns, rank), F32)],
    )
    coef = exchange(coef, 0)
    (near,) = run(
        near_field, [dense, ratings], [(users, columns)], "near_field", 6 * users * users * columns
    )
    lifted = run(
        functools.partial(up_split, 0, 0),
        [*coef, transfers],
        [(slim, rank)] * 4,
        "lift_leaves",
        unit * columns,
        [pltpu.VMEM((quarter, rank), F32)],
    )
    lifted = exchange(lifted, 1)
    leaf_fields = run(
        functools.partial(couple_all, 0, 0),
        [*coef, couplings],
        [(quarter, rank)] * 4,
        "couple_leaves",
        unit * 3 * columns,
    )
    (crown,) = run(
        functools.partial(up_last, 1, 1),
        [*lifted, transfers],
        [(slim, rank)],
        "lift_nodes",
        unit * quarter,
    )
    crown = exchange([crown] * 4, 2)
    node_fields = run(
        functools.partial(couple_all, 1, 1),
        [*lifted, couplings],
        [(slim, rank)] * 4,
        "couple_nodes",
        unit * 3 * quarter,
    )
    node_g = run(
        top,
        [*crown, couplings, transfers, *node_fields],
        [(slim, rank)] * 4,
        "top",
        unit * 7 * slim,
    )
    node_g = exchange(node_g, 1)
    leaf_g = run(
        down,
        [*node_g, transfers, *leaf_fields],
        [(quarter, rank)] * 4,
        "down",
        unit * columns,
        [pltpu.VMEM((quarter, rank), F32)],
    )
    leaf_g = exchange(leaf_g, 0)
    ins = [
        pltpu.with_memory_space_constraint(x, pltpu.VMEM) for x in (near, rbasis, *leaf_g)
    ]
    steps = 4
    return pl.pallas_call(
        finish,
        out_shape=jax.ShapeDtypeStruct((users, columns), F32),
        grid=(steps,),
        in_specs=[pl.BlockSpec(memory_space=pltpu.VMEM)] * 6,
        out_specs=pl.BlockSpec((users // steps, columns), lambda i: (i, 0)),
        scratch_shapes=[pltpu.VMEM((columns, rank), F32)],
        compiler_params=pltpu.CompilerParams(vmem_limit_bytes=16 * MIB),
        cost_estimate=pl.CostEstimate(
            flops=6 * users * rank * columns, bytes_accessed=4 * users * columns, transcendentals=0
        ),
        name="finish",
    )(*ins)


def solution(mesh):
    placed = (
        P("leaf", "col"),
        P("leaf", None, None),
        P("leaf", None, None),
        P("leaf", None, None),
        P(),
        P(),
    )
    return jax.shard_map(
        local, mesh=mesh, in_specs=placed, out_specs=P("leaf", "col"), check_vma=False
    )
```

```python
import functools

import jax
import jax.numpy as jnp
from jax import lax
from jax.experimental import pallas as pl
from jax.experimental.pallas import tpu as pltpu
from jax.sharding import PartitionSpec as P

F32 = jnp.float32
HIGH = lax.Precision.HIGH
MIB = 1 << 20
VMEM = pl.BlockSpec(memory_space=pltpu.VMEM)
ANY = pl.BlockSpec(memory_space=pl.ANY)


def dot(a, b, ca, cb):
    return lax.dot_general(
        a, b, (((ca,), (cb,)), ((), ())), precision=HIGH, preferred_element_type=F32
    )


def cost(flops, size):
    return pl.CostEstimate(flops=flops, bytes_accessed=4 * size, transcendentals=0)


def run(body, ins, outs, name, flops, after=(), scratch=(), vmem=24):
    ins = [pltpu.with_memory_space_constraint(x, pltpu.VMEM) for x in ins]

    def kernel(*refs):
        body(*refs[: len(ins)], *refs[len(ins) + len(after) :])

    return pl.pallas_call(
        kernel,
        out_shape=[pltpu.VMEM(shape, F32) for shape in outs],
        in_specs=[VMEM] * len(ins) + [ANY] * len(after),
        out_specs=[VMEM] * len(outs),
        scratch_shapes=list(scratch),
        compiler_params=pltpu.CompilerParams(vmem_limit_bytes=vmem * MIB),
        cost_estimate=cost(flops, sum(x.size for x in ins)),
        name=name,
    )(*ins, *after)


def place():
    leaf = lax.axis_index("leaf")
    return leaf % 4, (leaf // 4) % 4, leaf // 16


def other(index, j):
    low, high = index % 2, index // 2
    low = 1 - low if j & 1 else low
    high = 1 - high if j & 2 else high
    return 2 * high + low


def rows(index, count):
    return pl.ds(pl.multiple_of(index * count, count), count)


CHUNKS = 4


def leaf_coefficients(x, basis, o0, o1, o2, o3, held, basis_held, whole, sems):
    p, _, _ = place()
    chunk = x.shape[0] // CHUNKS
    copies = []
    for i in range(CHUNKS):
        at = pl.ds(i * chunk, chunk)
        pair = (
            pltpu.make_async_copy(x.at[at], held.at[at], sems.at[0, i]),
            pltpu.make_async_copy(basis.at[at], basis_held.at[at], sems.at[1, i]),
        )
        for copy in pair:
            copy.start()
        copies.append(pair)
    for i, pair in enumerate(copies):
        at = pl.ds(i * chunk, chunk)
        for copy in pair:
            copy.wait()
        term = dot(held[at, :], basis_held[at, :], 0, 0)
        whole[...] = term if i == 0 else whole[...] + term
    step = o0.shape[0]
    for j, out in enumerate((o0, o1, o2, o3)):
        out[...] = whole[rows(other(p, j), step), :]


def near_field(dense, x, out):
    @pl.loop(0, 4)
    def _(i):
        at = rows(i, 256)
        out[at, :] = dot(dense[at, :], x[...], 1, 0)


def lift(digit, level, c0, c1, c2, c3, transfers, out):
    own = place()[digit]
    total = None
    for j, c in enumerate((c0, c1, c2, c3)):
        term = dot(c[...], transfers[level, other(own, j)], 1, 0)
        total = term if total is None else total + term
    out[...] = total


def field_of(target, own, parts, level, couplings):
    at = other(own, target)
    total = None
    for j, c in enumerate(parts):
        if j == target:
            continue
        offset = (other(own, j) - at + 4) % 4
        term = dot(c[...], couplings[level, offset - 1], 1, 1)
        total = term if total is None else total + term
    return total


def couple(digit, level, c0, c1, c2, c3, couplings, *fields):
    own = place()[digit]
    for target, out in enumerate(fields):
        out[...] = field_of(target, own, (c0, c1, c2, c3), level, couplings)


def descend(c0, c1, c2, c3, couplings, transfers, field, f0, f1, f2, f3, o0, o1, o2, o3):
    p, q, r = place()
    g = field_of(0, r, (c0, c1, c2, c3), 2, couplings)
    g = field[...] + dot(g, transfers[1, q], 1, 1)
    for j, (f, out) in enumerate(zip((f0, f1, f2, f3), (o0, o1, o2, o3))):
        out[...] = f[...] + dot(g, transfers[0, other(p, j)], 1, 1)


def finish(half, near, row_basis, g0, g1, *rest):
    out, block, whole, sems = rest[-4:]
    p, _, _ = place()
    step = g0.shape[0]
    for j, g in enumerate((g0, g1)):
        whole[rows(other(p, j) % 2, step), :] = g[...]
    side = p // 2 if half == 0 else 1 - p // 2
    columns = rows(side, 2 * step)
    chunk = out.shape[0] // CHUNKS
    copies = []
    for i in range(CHUNKS):
        at = pl.ds(i * chunk, chunk)
        block[at, :] = near[at, columns] + dot(row_basis[at, :], whole[...], 1, 1)
        copy = pltpu.make_async_copy(block.at[at], out.at[at, columns], sems.at[i])
        copy.start()
        copies.append(copy)
    for copy in copies:
        copy.wait()


def swap(block, bits):
    count = lax.axis_size("leaf")
    return lax.ppermute(block, "leaf", [(i, i ^ bits) for i in range(count)])


def exchange(blocks, digit, order=(2, 3, 1)):
    got = {j: swap(blocks[j], j << 2 * digit) for j in order}
    return [blocks[0]] + [got[j] for j in (1, 2, 3)]


def local(ratings, dense_blocks, row_basis, col_basis, transfers, couplings):
    users, columns = ratings.shape
    rank = col_basis.shape[2]
    quarter = columns // 4
    unit = 2 * 3 * rank * rank
    dense, rbasis, cbasis = dense_blocks[0], row_basis[0], col_basis[0]

    *coef, held = pl.pallas_call(
        leaf_coefficients,
        out_shape=[pltpu.VMEM((quarter, rank), F32)] * 4 + [pltpu.VMEM((users, columns), F32)],
        in_specs=[ANY] * 2,
        out_specs=[VMEM] * 5,
        scratch_shapes=[
            pltpu.VMEM((users, rank), F32),
            pltpu.VMEM((columns, rank), F32),
            pltpu.SemaphoreType.DMA((2, CHUNKS)),
        ],
        compiler_params=pltpu.CompilerParams(vmem_limit_bytes=24 * MIB),
        cost_estimate=cost(6 * users * columns * rank, users * columns),
        name="leaf_coefficients",
    )(*[pltpu.with_memory_space_constraint(x, pltpu.HBM) for x in (ratings, cbasis)])
    coef = exchange(coef, 0)
    (near,) = run(
        near_field, [dense, held], [(users, columns)], "near_field", 6 * users * users * columns
    )
    (lifted,) = run(
        functools.partial(lift, 0, 0),
        [*coef, transfers],
        [(quarter, rank)],
        "lift_leaves",
        unit * columns,
        after=[near],
    )
    lifted = exchange([lifted] * 4, 1, (1, 3, 2))
    leaf_fields = run(
        functools.partial(couple, 0, 0),
        [*coef, couplings],
        [(quarter, rank)] * 4,
        "couple_leaves",
        unit * 3 * columns,
    )
    (crown,) = run(
        functools.partial(lift, 1, 1),
        [*lifted, transfers],
        [(quarter, rank)],
        "lift_nodes",
        unit * columns,
        after=leaf_fields,
    )
    crown = exchange([crown] * 4, 2, (1, 3, 2))
    (node_field,) = run(
        functools.partial(couple, 1, 1),
        [*lifted, couplings],
        [(quarter, rank)],
        "couple_nodes",
        unit * 3 * quarter,
    )
    leaf_g = run(
        descend,
        [*crown, couplings, transfers, node_field, *leaf_fields],
        [(quarter, rank)] * 4,
        "descend",
        unit * 8 * quarter,
    )
    leaf_g = exchange(leaf_g, 0)

    def half(which, pieces, out):
        ins = [
            pltpu.with_memory_space_constraint(x, pltpu.VMEM) for x in (near, rbasis, *pieces)
        ]
        return pl.pallas_call(
            functools.partial(finish, which),
            out_shape=pltpu.HBM((users, columns), F32),
            in_specs=[VMEM] * 4 + [ANY] * len(out),
            out_specs=ANY,
            scratch_shapes=[
                pltpu.VMEM((users, columns // 2), F32),
                pltpu.VMEM((columns // 2, rank), F32),
                pltpu.SemaphoreType.DMA((CHUNKS,)),
            ],
            input_output_aliases={4: 0} if out else {},
            compiler_params=pltpu.CompilerParams(vmem_limit_bytes=24 * MIB),
            cost_estimate=cost(3 * users * rank * columns, users * columns),
            name=("finish_own", "finish_other")[which],
        )(*ins, *out)

    out = half(0, leaf_g[:2], [])
    return half(1, leaf_g[2:], [out])


def solution(mesh):
    placed = (
        P("leaf", "col"),
        P("leaf", None, None),
        P("leaf", None, None),
        P("leaf", None, None),
        P(),
        P(),
    )
    return jax.shard_map(
        local, mesh=mesh, in_specs=placed, out_specs=P("leaf", "col"), check_vma=False
    )
```

```python
import functools

import jax
import jax.numpy as jnp
from jax import lax
from jax.experimental import pallas as pl
from jax.experimental.pallas import tpu as pltpu
from jax.sharding import PartitionSpec as P


F32 = jnp.float32
HIGH = lax.Precision.HIGH
MIB = 1 << 20
VMEM = pl.BlockSpec(memory_space=pltpu.VMEM)
ANY = pl.BlockSpec(memory_space=pl.ANY)
CHUNKS = 4


def dot(a, b, ca, cb):
    return lax.dot_general(
        a, b, (((ca,), (cb,)), ((), ())), precision=HIGH, preferred_element_type=F32
    )


def in_vmem(arrays):
    return [pltpu.with_memory_space_constraint(x, pltpu.VMEM) for x in arrays]


def in_hbm(arrays):
    return [pltpu.with_memory_space_constraint(x, pltpu.HBM) for x in arrays]


def settings(flops, size, name):
    return dict(
        compiler_params=pltpu.CompilerParams(vmem_limit_bytes=24 * MIB),
        cost_estimate=pl.CostEstimate(flops=flops, bytes_accessed=4 * size, transcendentals=0),
        name=name,
    )


def run(body, ins, outs, name, flops, after=(), scratch=()):
    def kernel(*refs):
        body(*refs[: len(ins)], *refs[len(ins) + len(after) :])

    return pl.pallas_call(
        kernel,
        out_shape=[pltpu.VMEM(shape, F32) for shape in outs],
        in_specs=[VMEM] * len(ins) + [ANY] * len(after),
        out_specs=[VMEM] * len(outs),
        scratch_shapes=[pltpu.VMEM(shape, F32) for shape in scratch],
        **settings(flops, sum(x.size for x in ins), name),
    )(*in_vmem(ins), *after)


def place():
    leaf = lax.axis_index("leaf")
    return leaf // 16, leaf // 4 % 4, leaf % 4, leaf % 2


def span(index, count):
    return pl.ds(pl.multiple_of(index * count, count), count)


def pick(core, first, second):
    return jnp.where(core == 0, first[...], second[...])


def offset(source, target):
    return (source - target + 4) % 4 - 1


def far_coefficients(x, basis, o2, o3, held, basis_held, whole, sems, rest_sem):
    _, m, k, _ = place()
    users, wide = x.shape[0], x.shape[1] // 2
    chunk = users // CHUNKS
    far = 1 - (k ^ m) // 2
    columns = span(far, wide)
    copies = []
    for i in range(CHUNKS):
        at = pl.ds(i * chunk, chunk)
        pair = (
            pltpu.make_async_copy(basis.at[at], basis_held.at[at], sems.at[0, i]),
            pltpu.make_async_copy(x.at[at, columns], held.at[at, columns], sems.at[1, i]),
        )
        for copy in pair:
            copy.start()
        copies.append(pair)
    near_columns = span(1 - far, wide)
    rest = pltpu.make_async_copy(x.at[:, near_columns], held.at[:, near_columns], rest_sem)
    rest.start()
    for i, pair in enumerate(copies):
        at = pl.ds(i * chunk, chunk)
        for copy in pair:
            copy.wait()
        term = dot(held[at, columns], basis_held[at, :], 0, 0)
        whole[...] = term if i == 0 else whole[...] + term
    for j, out in ((2, o2), (3, o3)):
        out[...] = whole[span((k ^ m ^ j) % 2, wide // 2), :]
    rest.wait()


def own_coefficients(held, basis_held, o0, o1, whole):
    _, m, k, _ = place()
    wide = held.shape[1] // 2
    whole[...] = dot(held[:, span((k ^ m) // 2, wide)], basis_held[...], 0, 0)
    for j, out in ((0, o0), (1, o1)):
        out[...] = whole[span((k ^ m ^ j) % 2, wide // 2), :]


def near_field(dense, x, out, held, sems):
    chunk = dense.shape[0] // CHUNKS
    copies = []
    for i in range(CHUNKS):
        at = pl.ds(i * chunk, chunk)
        copy = pltpu.make_async_copy(dense.at[at], held.at[at], sems.at[i])
        copy.start()
        copies.append(copy)
    for i, copy in enumerate(copies):
        at = pl.ds(i * chunk, chunk)
        copy.wait()
        out[at, :] = dot(held[at, :], x[...], 1, 0)


def split_out(core, m, whole, a, rest):
    step = a.shape[0]
    a[...] = whole[span((m // 2 + 1 - core) % 2, step), :]
    rest[...] = whole[span((m // 2 + core) % 2, step), :]


def lift_leaves(c0, c1, c2, c3, transfers, a, rest, whole):
    _, m, k, core = place()
    whole[...] = (
        dot(c0[...], transfers[0, k], 1, 0)
        + dot(c1[...], transfers[0, k ^ 1], 1, 0)
        + dot(c2[...], transfers[0, k ^ 2], 1, 0)
        + dot(c3[...], transfers[0, k ^ 3], 1, 0)
    )
    split_out(core, m, whole, a, rest)


def couple_leaves(c0, c1, c2, c3, couplings, *fields):
    k = place()[2]
    parts = (c0, c1, c2, c3)
    for target, out in enumerate(fields):
        at = k ^ target
        out[...] = sum(
            dot(parts[target ^ d][...], couplings[0, offset(at ^ d, at)], 1, 1) for d in (1, 2, 3)
        )


def lift_nodes(rest, a, b, swapped_rest, swapped_a, swapped_b, transfers, out, parts):
    _, m, _, core = place()
    step = out.shape[0]
    blocks = (
        pick(core, rest, swapped_rest),
        pick(core, swapped_a, a),
        pick(core, a, swapped_a),
        pick(core, swapped_b, b),
    )
    total = None
    for j, block in enumerate(blocks):
        parts[pl.ds(j * step, step), :] = block
        term = dot(block, transfers[1, m ^ j], 1, 0)
        total = term if total is None else total + term
    out[...] = total


def couple_nodes(parts, couplings, a, rest):
    _, m, _, core = place()
    step = a.shape[0]
    for target, out in ((2 - core, a), (3 * core, rest)):
        at = m ^ target
        out[...] = sum(
            dot(parts[span(target ^ d, step), :], couplings[1, offset(at ^ d, at)], 1, 1)
            for d in (1, 2, 3)
        )


def top(a, b, swapped_a, swapped_b, couplings, transfers, field_a, field_rest, out_a, out_rest):
    r, m, _, core = place()
    blocks = (pick(core, swapped_a, a), pick(core, a, swapped_a), pick(core, swapped_b, b))
    g = sum(
        dot(block, couplings[2, offset(r ^ d, r)], 1, 1) for d, block in zip((1, 2, 3), blocks)
    )
    out_a[...] = field_a[...] + dot(g, transfers[1, m ^ (2 - core)], 1, 1)
    out_rest[...] = field_rest[...] + dot(g, transfers[1, m ^ (3 * core)], 1, 1)


def descend(rest, a, b, transfers, f0, f1, f2, f3, o0, o1, o2, o3, whole):
    _, m, k, core = place()
    step = a.shape[0]
    whole[span(m // 2, step), :] = pick(core, rest, a)
    whole[span(1 - m // 2, step), :] = pick(core, a, b)
    g = whole[...]
    for j, (field, out) in enumerate(((f0, o0), (f1, o1), (f2, o2), (f3, o3))):
        out[...] = field[...] + dot(g, transfers[0, k ^ j], 1, 1)


def finish(first, near, row_basis, *rest):
    out, block, whole, sems = rest[-4:]
    _, m, k, _ = place()
    wide, step = whole.shape[0], rest[0].shape[0]
    if wide == step:
        whole[...] = rest[0][...]
        columns = span(k ^ m ^ first, wide)
    else:
        for j in (0, 1):
            whole[span((k ^ m ^ j) % 2, step), :] = rest[j][...]
        columns = span((k ^ m ^ first) // 2, wide)
    chunk = out.shape[0] // CHUNKS
    copies = []
    for i in range(CHUNKS):
        at = pl.ds(i * chunk, chunk)
        block[at, :] = near[at, columns] + dot(row_basis[at, :], whole[...], 1, 1)
        copy = pltpu.make_async_copy(block.at[at], out.at[at, columns], sems.at[i])
        copy.start()
        copies.append(copy)
    for copy in copies:
        copy.wait()


def send(block, target):
    pairs = [(i, target(i, i % 2)) for i in range(lax.axis_size("leaf"))]
    return lax.ppermute(block, "leaf", [pair for pair in pairs if pair[1] is not None])


def swap(block, bits):
    return send(block, lambda i, core: i ^ bits)


def to_nodes(a, rest):
    got_a = send(a, lambda i, core: i ^ (4 if core else 10))
    return got_a, send(rest, lambda i, core: i ^ 14 if core else None)


def to_tops(block):
    got_a = send(block, lambda i, core: i ^ (16 if core else 32))
    return got_a, send(block, lambda i, core: i ^ 48 if core else None)


def to_core_0(block):
    return send(block, lambda i, core: i ^ 1 if core else None)


def to_core_1(block):
    return send(block, lambda i, core: None if core else i ^ 1)


def local(ratings, dense_blocks, row_basis, col_basis, transfers, couplings):
    users, columns = ratings.shape
    rank = col_basis.shape[2]
    quarter, slim = columns // 4, columns // 8
    unit = 2 * 3 * rank * rank
    dense, rbasis, cbasis = dense_blocks[0], row_basis[0], col_basis[0]

    c2, c3, held, basis_held = pl.pallas_call(
        far_coefficients,
        out_shape=[
            pltpu.VMEM(shape, F32)
            for shape in ((quarter, rank), (quarter, rank), (users, columns), (users, rank))
        ],
        in_specs=[ANY] * 2,
        out_specs=[VMEM] * 4,
        scratch_shapes=[
            pltpu.VMEM((columns // 2, rank), F32),
            pltpu.SemaphoreType.DMA((2, CHUNKS)),
            pltpu.SemaphoreType.DMA,
        ],
        **settings(3 * users * columns * rank, users * columns, "far_coefficients"),
    )(*in_hbm([ratings, cbasis]))
    c2, c3 = swap(c2, 2), swap(c3, 3)
    c0, c1 = run(
        own_coefficients,
        [held, basis_held],
        [(quarter, rank)] * 2,
        "own_coefficients",
        3 * users * columns * rank,
        scratch=[(columns // 2, rank)],
    )
    c1 = swap(c1, 1)
    near = pl.pallas_call(
        near_field,
        out_shape=pltpu.VMEM((users, columns), F32),
        in_specs=[ANY, VMEM],
        out_specs=VMEM,
        scratch_shapes=[pltpu.VMEM((users, users), F32), pltpu.SemaphoreType.DMA((CHUNKS,))],
        **settings(6 * users * users * columns, users * users, "near_field"),
    )(*in_hbm([dense]), *in_vmem([held]))
    coef = [c0, c1, c2, c3]
    a, rest = run(
        lift_leaves,
        [*coef, transfers],
        [(slim, rank)] * 2,
        "lift_leaves",
        unit * columns,
        after=[near],
        scratch=[(quarter, rank)],
    )
    got_a, got_b = to_nodes(a, rest)
    swapped_rest = to_core_1(rest)
    leaf_fields = run(
        couple_leaves, [*coef, couplings], [(quarter, rank)] * 4, "couple_leaves", unit * 3 * columns
    )
    swapped_a, swapped_b = swap(got_a, 1), to_core_0(got_b)
    crown, parts = run(
        lift_nodes,
        [rest, got_a, got_b, swapped_rest, swapped_a, swapped_b, transfers],
        [(slim, rank), (4 * slim, rank)],
        "lift_nodes",
        unit * 4 * slim,
    )
    got_a, got_b = to_tops(crown)
    node_fields = run(
        couple_nodes, [parts, couplings], [(slim, rank)] * 2, "couple_nodes", unit * 6 * slim
    )
    a, rest = run(
        top,
        [got_a, got_b, swap(got_a, 1), to_core_0(got_b), couplings, transfers, *node_fields],
        [(slim, rank)] * 2,
        "top",
        unit * 5 * slim,
    )
    got_a, got_b = to_nodes(a, rest)

    g0, g1, g2, g3 = run(
        descend,
        [rest, got_a, got_b, transfers, *leaf_fields],
        [(quarter, rank)] * 4,
        "descend",
        unit * columns,
        scratch=[(quarter, rank)],
    )
    g2, g3, g1 = swap(g2, 2), swap(g3, 3), swap(g1, 1)

    def write(first, pieces, out):
        wide = len(pieces) * quarter
        return pl.pallas_call(
            functools.partial(finish, first),
            out_shape=pltpu.HBM((users, columns), F32),
            in_specs=[VMEM] * (2 + len(pieces)) + [ANY] * len(out),
            out_specs=ANY,
            scratch_shapes=[
                pltpu.VMEM((users, wide), F32),
                pltpu.VMEM((wide, rank), F32),
                pltpu.SemaphoreType.DMA((CHUNKS,)),
            ],
            input_output_aliases={2 + len(pieces): 0} if out else {},
            **settings(6 * users * rank * wide, users * wide, "finish_%d" % first),
        )(*in_vmem([near, rbasis, *pieces]), *out)

    out = write(0, [g0, g1], [])
    out = write(2, [g2], [out])
    return write(3, [g3], [out])


def solution(mesh):
    placed = (
        P("leaf", "col"),
        P("leaf", None, None),
        P("leaf", None, None),
        P("leaf", None, None),
        P(),
        P(),
    )
    return jax.shard_map(
        local, mesh=mesh, in_specs=placed, out_specs=P("leaf", "col"), check_vma=False
    )
```

```python
import functools

import jax
import jax.numpy as jnp
from jax import lax
from jax.experimental import pallas as pl
from jax.experimental.pallas import tpu as pltpu
from jax.sharding import PartitionSpec as P


F32 = jnp.float32
HIGH = lax.Precision.HIGH
MIB = 1 << 20
VMEM = pl.BlockSpec(memory_space=pltpu.VMEM)
ANY = pl.BlockSpec(memory_space=pl.ANY)
CHUNKS = 4


def dot(a, b, ca, cb):
    return lax.dot_general(
        a, b, (((ca,), (cb,)), ((), ())), precision=HIGH, preferred_element_type=F32
    )


def in_vmem(arrays):
    return [pltpu.with_memory_space_constraint(x, pltpu.VMEM) for x in arrays]


def in_hbm(arrays):
    return [pltpu.with_memory_space_constraint(x, pltpu.HBM) for x in arrays]


def settings(flops, size, name):
    return dict(
        compiler_params=pltpu.CompilerParams(vmem_limit_bytes=24 * MIB),
        cost_estimate=pl.CostEstimate(flops=flops, bytes_accessed=4 * size, transcendentals=0),
        name=name,
    )


def run(body, ins, outs, name, flops, after=(), scratch=()):
    def kernel(*refs):
        body(*refs[: len(ins)], *refs[len(ins) + len(after) :])

    return pl.pallas_call(
        kernel,
        out_shape=[pltpu.VMEM(shape, F32) for shape in outs],
        in_specs=[VMEM] * len(ins) + [ANY] * len(after),
        out_specs=[VMEM] * len(outs),
        scratch_shapes=[pltpu.VMEM(shape, F32) for shape in scratch],
        **settings(flops, sum(x.size for x in ins), name),
    )(*in_vmem(ins), *after)


def place():
    leaf = lax.axis_index("leaf")
    return leaf // 16, leaf // 4 % 4, leaf % 4, leaf % 2


def span(index, count):
    return pl.ds(pl.multiple_of(index * count, count), count)


def pick(core, first, second):
    return jnp.where(core == 0, first[...], second[...])


def offset(source, target):
    return (source - target + 4) % 4 - 1


def far_coefficients(x, basis, o2, o3, held, basis_held, whole, sems, rest_sem):
    _, m, k, _ = place()
    users, wide = x.shape[0], x.shape[1] // 2
    chunk = users // CHUNKS
    far = 1 - (k ^ m) // 2
    columns = span(far, wide)
    copies = []
    for i in range(CHUNKS):
        at = pl.ds(i * chunk, chunk)
        pair = (
            pltpu.make_async_copy(basis.at[at], basis_held.at[at], sems.at[0, i]),
            pltpu.make_async_copy(x.at[at, columns], held.at[at, columns], sems.at[1, i]),
        )
        for copy in pair:
            copy.start()
        copies.append(pair)
    near_columns = span(1 - far, wide)
    rest = pltpu.make_async_copy(x.at[:, near_columns], held.at[:, near_columns], rest_sem)
    rest.start()
    for i, pair in enumerate(copies):
        at = pl.ds(i * chunk, chunk)
        for copy in pair:
            copy.wait()
        term = dot(held[at, columns], basis_held[at, :], 0, 0)
        whole[...] = term if i == 0 else whole[...] + term
    for j, out in ((2, o2), (3, o3)):
        out[...] = whole[span((k ^ m ^ j) % 2, wide // 2), :]
    rest.wait()


def own_and_near(held, basis_held, dense, o0, o1, out, dense_rest, whole, dense_held, sems):
    _, m, k, _ = place()
    wide = held.shape[1] // 2
    users = dense.shape[0]
    chunk = users // (2 * CHUNKS)
    copies = []
    for i in range(CHUNKS):
        at = pl.ds(i * chunk, chunk)
        copies.append(pltpu.make_async_copy(dense.at[at], dense_held.at[at], sems.at[i]))
    below = pl.ds(users // 2, users // 2)
    copies.append(pltpu.make_async_copy(dense.at[below], dense_rest, sems.at[CHUNKS]))
    for copy in copies:
        copy.start()
    whole[...] = dot(held[:, span((k ^ m) // 2, wide)], basis_held[...], 0, 0)
    for j, piece in ((0, o0), (1, o1)):
        piece[...] = whole[span((k ^ m ^ j) % 2, wide // 2), :]
    for i in range(CHUNKS):
        at = pl.ds(i * chunk, chunk)
        copies[i].wait()
        out[at, :] = dot(dense_held[at, :], held[...], 1, 0)
    copies[CHUNKS].wait()


def near_field(dense, x, out):
    half = dense.shape[0] // 2
    for i in range(2):
        at = pl.ds(i * half, half)
        out[at, :] = dot(dense[at, :], x[...], 1, 0)


def split_out(core, m, whole, a, rest):
    step = a.shape[0]
    a[...] = whole[span((m // 2 + 1 - core) % 2, step), :]
    rest[...] = whole[span((m // 2 + core) % 2, step), :]


def lift_leaves(c0, c1, c2, c3, transfers, a, rest, whole):
    _, m, k, core = place()
    whole[...] = (
        dot(c0[...], transfers[0, k], 1, 0)
        + dot(c1[...], transfers[0, k ^ 1], 1, 0)
        + dot(c2[...], transfers[0, k ^ 2], 1, 0)
        + dot(c3[...], transfers[0, k ^ 3], 1, 0)
    )
    split_out(core, m, whole, a, rest)


def couple_leaves(c0, c1, c2, c3, couplings, *fields):
    k = place()[2]
    parts = (c0, c1, c2, c3)
    for target, out in enumerate(fields):
        at = k ^ target
        out[...] = sum(
            dot(parts[target ^ d][...], couplings[0, offset(at ^ d, at)], 1, 1) for d in (1, 2, 3)
        )


def lift_nodes(a, b, swapped_a, swapped_b, transfers, out, parts):
    _, m, _, core = place()
    step = out.shape[0]
    blocks = (
        pick(core, b, swapped_b),
        pick(core, swapped_a, a),
        pick(core, a, swapped_a),
        pick(core, swapped_b, b),
    )
    total = None
    for j, block in enumerate(blocks):
        parts[pl.ds(j * step, step), :] = block
        term = dot(block, transfers[1, m ^ j], 1, 0)
        total = term if total is None else total + term
    out[...] = total


def couple_nodes(parts, couplings, a, rest):
    _, m, _, core = place()
    step = a.shape[0]
    for target, out in ((2 - core, a), (3 * core, rest)):
        at = m ^ target
        out[...] = sum(
            dot(parts[span(target ^ d, step), :], couplings[1, offset(at ^ d, at)], 1, 1)
            for d in (1, 2, 3)
        )


def top(a, b, swapped_a, swapped_b, couplings, transfers, field_a, field_rest, out_a, out_rest):
    r, m, _, core = place()
    blocks = (pick(core, swapped_a, a), pick(core, a, swapped_a), pick(core, swapped_b, b))
    g = sum(
        dot(block, couplings[2, offset(r ^ d, r)], 1, 1) for d, block in zip((1, 2, 3), blocks)
    )
    out_a[...] = field_a[...] + dot(g, transfers[1, m ^ (2 - core)], 1, 1)
    out_rest[...] = field_rest[...] + dot(g, transfers[1, m ^ (3 * core)], 1, 1)


def descend(a, b, transfers, f0, f1, f2, f3, o0, o1, o2, o3, whole):
    _, m, k, core = place()
    step = a.shape[0]
    whole[span(m // 2, step), :] = pick(core, b, a)
    whole[span(1 - m // 2, step), :] = pick(core, a, b)
    g = whole[...]
    for j, (field, out) in enumerate(((f0, o0), (f1, o1), (f2, o2), (f3, o3))):
        out[...] = field[...] + dot(g, transfers[0, k ^ j], 1, 1)


def finish(first, near_above, near_below, row_basis, *rest):
    out, block, whole, sems = rest[-4:]
    _, m, k, _ = place()
    wide, step = whole.shape[0], rest[0].shape[0]
    if wide == step:
        whole[...] = rest[0][...]
        columns = span(k ^ m ^ first, wide)
    else:
        for j in (0, 1):
            whole[span((k ^ m ^ j) % 2, step), :] = rest[j][...]
        columns = span((k ^ m ^ first) // 2, wide)
    chunk = out.shape[0] // CHUNKS
    copies = []
    for i in range(CHUNKS):
        at = pl.ds(i * chunk, chunk)
        near = near_above if 2 * i < CHUNKS else near_below
        part = near[pl.ds(i * chunk % near.shape[0], chunk), columns]
        block[at, :] = part + dot(row_basis[at, :], whole[...], 1, 1)
        copy = pltpu.make_async_copy(block.at[at], out.at[at, columns], sems.at[i])
        copy.start()
        copies.append(copy)
    for copy in copies:
        copy.wait()


def send(block, target):
    return lax.ppermute(
        block, "leaf", [(i, target(i, i % 2)) for i in range(lax.axis_size("leaf"))]
    )


def swap(block, bits):
    return send(block, lambda i, core: i ^ bits)


def to_nodes(a, rest):
    return send(a, lambda i, core: i ^ (4 if core else 10)), send(
        rest, lambda i, core: i ^ (14 if core else 0)
    )


def to_tops(block):
    return send(block, lambda i, core: i ^ (16 if core else 32)), send(
        block, lambda i, core: i ^ (48 if core else 0)
    )


def local(ratings, dense_blocks, row_basis, col_basis, transfers, couplings):
    users, columns = ratings.shape
    rank = col_basis.shape[2]
    quarter, slim = columns // 4, columns // 8
    unit = 2 * 3 * rank * rank
    dense, rbasis, cbasis = dense_blocks[0], row_basis[0], col_basis[0]

    c2, c3, held, basis_held = pl.pallas_call(
        far_coefficients,
        out_shape=[
            pltpu.VMEM(shape, F32)
            for shape in ((quarter, rank), (quarter, rank), (users, columns), (users, rank))
        ],
        in_specs=[ANY] * 2,
        out_specs=[VMEM] * 4,
        scratch_shapes=[
            pltpu.VMEM((columns // 2, rank), F32),
            pltpu.SemaphoreType.DMA((2, CHUNKS)),
            pltpu.SemaphoreType.DMA,
        ],
        **settings(3 * users * columns * rank, users * columns, "far_coefficients"),
    )(*in_hbm([ratings, cbasis]))
    c2, c3 = swap(c2, 2), swap(c3, 3)
    c0, c1, near_above, dense_rest = pl.pallas_call(
        own_and_near,
        out_shape=[
            pltpu.VMEM(shape, F32)
            for shape in (
                (quarter, rank),
                (quarter, rank),
                (users // 2, columns),
                (users // 2, users),
            )
        ],
        in_specs=[VMEM, VMEM, ANY],
        out_specs=[VMEM] * 4,
        scratch_shapes=[
            pltpu.VMEM((columns // 2, rank), F32),
            pltpu.VMEM((users // 2, users), F32),
            pltpu.SemaphoreType.DMA((CHUNKS + 1,)),
        ],
        **settings(3 * users * users * columns, users * users, "own_and_near"),
    )(*in_vmem([held, basis_held]), *in_hbm([dense]))
    c1 = swap(c1, 1)
    (near_below,) = run(
        near_field,
        [dense_rest, held],
        [(users // 2, columns)],
        "near_field",
        3 * users * users * columns,
    )
    coef = [c0, c1, c2, c3]
    a, rest = run(
        lift_leaves,
        [*coef, transfers],
        [(slim, rank)] * 2,
        "lift_leaves",
        unit * columns,
        scratch=[(quarter, rank)],
    )
    got_a, got_b = to_nodes(a, rest)
    leaf_fields = run(
        couple_leaves, [*coef, couplings], [(quarter, rank)] * 4, "couple_leaves", unit * 3 * columns
    )
    swapped_a, swapped_b = swap(got_a, 1), swap(got_b, 1)
    crown, parts = run(
        lift_nodes,
        [got_a, got_b, swapped_a, swapped_b, transfers],
        [(slim, rank), (4 * slim, rank)],
        "lift_nodes",
        unit * 4 * slim,
    )
    got_a, got_b = to_tops(crown)
    node_fields = run(
        couple_nodes, [parts, couplings], [(slim, rank)] * 2, "couple_nodes", unit * 6 * slim
    )
    a, rest = run(
        top,
        [got_a, got_b, swap(got_a, 1), swap(got_b, 1), couplings, transfers, *node_fields],
        [(slim, rank)] * 2,
        "top",
        unit * 5 * slim,
    )
    got_a, got_b = to_nodes(a, rest)

    g0, g1, g2, g3 = run(
        descend,
        [got_a, got_b, transfers, *leaf_fields],
        [(quarter, rank)] * 4,
        "descend",
        unit * columns,
        scratch=[(quarter, rank)],
    )
    g2, g3, g1 = swap(g2, 2), swap(g3, 3), swap(g1, 1)

    def write(first, pieces, out):
        wide = len(pieces) * quarter
        return pl.pallas_call(
            functools.partial(finish, first),
            out_shape=pltpu.HBM((users, columns), F32),
            in_specs=[VMEM] * (3 + len(pieces)) + [ANY] * len(out),
            out_specs=ANY,
            scratch_shapes=[
                pltpu.VMEM((users, wide), F32),
                pltpu.VMEM((wide, rank), F32),
                pltpu.SemaphoreType.DMA((CHUNKS,)),
            ],
            input_output_aliases={3 + len(pieces): 0} if out else {},
            **settings(6 * users * rank * wide, users * wide, "finish_%d" % first),
        )(*in_vmem([near_above, near_below, rbasis, *pieces]), *out)

    out = write(0, [g0, g1], [])
    out = write(2, [g2], [out])
    return write(3, [g3], [out])


def solution(mesh):
    placed = (
        P("leaf", "col"),
        P("leaf", None, None),
        P("leaf", None, None),
        P("leaf", None, None),
        P(),
        P(),
    )
    return jax.shard_map(
        local, mesh=mesh, in_specs=placed, out_specs=P("leaf", "col"), check_vma=False
    )
```

```python
import functools

import jax
import jax.numpy as jnp
from jax import lax
from jax.experimental import pallas as pl
from jax.experimental.pallas import tpu as pltpu
from jax.sharding import PartitionSpec as P


F32 = jnp.float32
HIGH = lax.Precision.HIGH
MIB = 1 << 20
VMEM = pl.BlockSpec(memory_space=pltpu.VMEM)
ANY = pl.BlockSpec(memory_space=pl.ANY)
CHUNKS = 4


def dot(a, b, ca, cb):
    return lax.dot_general(
        a, b, (((ca,), (cb,)), ((), ())), precision=HIGH, preferred_element_type=F32
    )


def in_vmem(arrays):
    return [pltpu.with_memory_space_constraint(x, pltpu.VMEM) for x in arrays]


def in_hbm(arrays):
    return [pltpu.with_memory_space_constraint(x, pltpu.HBM) for x in arrays]


def settings(flops, size, name):
    return dict(
        compiler_params=pltpu.CompilerParams(vmem_limit_bytes=24 * MIB),
        cost_estimate=pl.CostEstimate(flops=flops, bytes_accessed=4 * size, transcendentals=0),
        name=name,
    )


def run(body, ins, outs, name, flops, after=(), scratch=()):
    def kernel(*refs):
        body(*refs[: len(ins)], *refs[len(ins) + len(after) :])

    return pl.pallas_call(
        kernel,
        out_shape=[pltpu.VMEM(shape, F32) for shape in outs],
        in_specs=[VMEM] * len(ins) + [ANY] * len(after),
        out_specs=[VMEM] * len(outs),
        scratch_shapes=[pltpu.VMEM(shape, F32) for shape in scratch],
        **settings(flops, sum(x.size for x in ins), name),
    )(*in_vmem(ins), *after)


def place():
    leaf = lax.axis_index("leaf")
    return leaf // 16, leaf // 4 % 4, leaf % 4, leaf % 2


def span(index, count):
    return pl.ds(pl.multiple_of(index * count, count), count)


def pick(core, first, second):
    return jnp.where(core == 0, first[...], second[...])


def offset(source, target):
    return (source - target + 4) % 4 - 1


def far_coefficients(x, basis, o2, o3, held, basis_held, whole, sems):
    _, m, k, _ = place()
    users, wide = x.shape[0], x.shape[1] // 2
    chunk = users // CHUNKS
    columns = span(1 - (k ^ m) // 2, wide)
    copies = []
    for i in range(CHUNKS):
        at = pl.ds(i * chunk, chunk)
        pair = (
            pltpu.make_async_copy(basis.at[at], basis_held.at[at], sems.at[0, i]),
            pltpu.make_async_copy(x.at[at, columns], held.at[at], sems.at[1, i]),
        )
        for copy in pair:
            copy.start()
        copies.append(pair)
    for i, pair in enumerate(copies):
        at = pl.ds(i * chunk, chunk)
        for copy in pair:
            copy.wait()
        term = dot(held[at, :], basis_held[at, :], 0, 0)
        whole[...] = term if i == 0 else whole[...] + term
    for j, out in ((2, o2), (3, o3)):
        out[...] = whole[span((k ^ m ^ j) % 2, wide // 2), :]


def own_and_near(
    far, basis_held, x, dense, o0, o1, out, dense_rest, held, whole, dense_held, sems, x_sem
):
    _, m, k, _ = place()
    users, wide = x.shape[0], x.shape[1] // 2
    own = span((k ^ m) // 2, wide)
    own_copy = pltpu.make_async_copy(x.at[:, own], held.at[:, own], x_sem)
    own_copy.start()
    chunk = users // (2 * CHUNKS)
    copies = []
    for i in range(CHUNKS):
        at = pl.ds(i * chunk, chunk)
        copies.append(pltpu.make_async_copy(dense.at[at], dense_held.at[at], sems.at[i]))
    below = pl.ds(users // 2, users // 2)
    copies.append(pltpu.make_async_copy(dense.at[below], dense_rest, sems.at[CHUNKS]))
    for copy in copies:
        copy.start()
    held[:, span(1 - (k ^ m) // 2, wide)] = far[...]
    own_copy.wait()
    whole[...] = dot(held[:, own], basis_held[...], 0, 0)
    for j, piece in ((0, o0), (1, o1)):
        piece[...] = whole[span((k ^ m ^ j) % 2, wide // 2), :]
    for i in range(CHUNKS):
        at = pl.ds(i * chunk, chunk)
        copies[i].wait()
        out[at, :] = dot(dense_held[at, :], held[...], 1, 0)
    copies[CHUNKS].wait()


def near_field(dense, x, out):
    half = dense.shape[0] // 2
    for i in range(2):
        at = pl.ds(i * half, half)
        out[at, :] = dot(dense[at, :], x[...], 1, 0)


def split_out(core, m, whole, a, rest):
    step = a.shape[0]
    a[...] = whole[span((m // 2 + 1 - core) % 2, step), :]
    rest[...] = whole[span((m // 2 + core) % 2, step), :]


def lift_leaves(c0, c1, c2, c3, transfers, a, rest, whole):
    _, m, k, core = place()
    whole[...] = (
        dot(c0[...], transfers[0, k], 1, 0)
        + dot(c1[...], transfers[0, k ^ 1], 1, 0)
        + dot(c2[...], transfers[0, k ^ 2], 1, 0)
        + dot(c3[...], transfers[0, k ^ 3], 1, 0)
    )
    split_out(core, m, whole, a, rest)


def couple_leaves(c0, c1, c2, c3, couplings, *fields):
    k = place()[2]
    parts = (c0, c1, c2, c3)
    for target, out in enumerate(fields):
        at = k ^ target
        out[...] = sum(
            dot(parts[target ^ d][...], couplings[0, offset(at ^ d, at)], 1, 1) for d in (1, 2, 3)
        )


def order(core, a, b, out):
    step = a.shape[0]
    out[pl.ds(0, step), :] = pick(core, b, a)
    out[pl.ds(step, step), :] = pick(core, a, b)


def merge(a, b, out):
    order(place()[3], a, b, out)


def merge_slices(a, b, out):
    _, m, _, core = place()
    step = a.shape[0]
    out[span(m // 2, step), :] = pick(core, b, a)
    out[span(1 - m // 2, step), :] = pick(core, a, b)


def relay(block, out):
    out[...] = block[...]


def all_blocks(core, ours, theirs):
    step = ours.shape[0] // 2
    for j in range(4):
        at = pl.ds(j // 2 * step, step)
        even, odd = (ours, theirs) if j % 2 == 0 else (theirs, ours)
        yield pick(core, even.at[at], odd.at[at])


def lift_nodes(ours, theirs, transfers, out, parts):
    _, m, _, core = place()
    step = out.shape[0]
    total = None
    for j, block in enumerate(all_blocks(core, ours, theirs)):
        parts[pl.ds(j * step, step), :] = block
        term = dot(block, transfers[1, m ^ j], 1, 0)
        total = term if total is None else total + term
    out[...] = total


def couple_nodes(parts, couplings, a, rest):
    _, m, _, core = place()
    step = a.shape[0]
    for target, out in ((2 - core, a), (3 * core, rest)):
        at = m ^ target
        out[...] = sum(
            dot(parts[span(target ^ d, step), :], couplings[1, offset(at ^ d, at)], 1, 1)
            for d in (1, 2, 3)
        )


def top(ours, theirs, couplings, transfers, field_a, field_rest, out_a, out_rest):
    r, m, _, core = place()
    g = sum(
        dot(block, couplings[2, offset(r ^ d, r)], 1, 1)
        for d, block in enumerate(all_blocks(core, ours, theirs))
        if d
    )
    out_a[...] = field_a[...] + dot(g, transfers[1, m ^ (2 - core)], 1, 1)
    out_rest[...] = field_rest[...] + dot(g, transfers[1, m ^ (3 * core)], 1, 1)


def finish(first, near_above, near_below, row_basis, transfers, *rest):
    *pieces, out, block, whole, sems = rest
    pieces = [pieces[i : i + 2] for i in range(0, len(pieces) - len(pieces) % 2, 2)]
    _, m, k, _ = place()
    wide, quarter = whole.shape[0], pieces[0][0].shape[0]
    for n, (field, parent) in enumerate(pieces):
        g = field[...] + dot(parent[...], transfers[0, k], 1, 1)
        whole[span((k ^ m ^ (first + n)) % (wide // quarter), quarter), :] = g
    columns = span((k ^ m ^ first) // (wide // quarter), wide)
    chunk = out.shape[0] // CHUNKS
    copies = []
    for i in range(CHUNKS):
        at = pl.ds(i * chunk, chunk)
        near = near_above if 2 * i < CHUNKS else near_below
        part = near[pl.ds(i * chunk % near.shape[0], chunk), columns]
        block[at, :] = part + dot(row_basis[at, :], whole[...], 1, 1)
        copy = pltpu.make_async_copy(block.at[at], out.at[at, columns], sems.at[i])
        copy.start()
        copies.append(copy)
    for copy in copies:
        copy.wait()


def send(block, target):
    return lax.ppermute(
        block, "leaf", [(i, target(i, i % 2)) for i in range(lax.axis_size("leaf"))]
    )


def swap(block, bits):
    return send(block, lambda i, core: i ^ bits)


def to_nodes(a, rest):
    return send(a, lambda i, core: i ^ (4 if core else 10)), send(
        rest, lambda i, core: i ^ (14 if core else 0)
    )


def to_tops(block):
    return send(block, lambda i, core: i ^ (16 if core else 32)), send(
        block, lambda i, core: i ^ (48 if core else 0)
    )


def local(ratings, dense_blocks, row_basis, col_basis, transfers, couplings):
    users, columns = ratings.shape
    rank = col_basis.shape[2]
    quarter, slim = columns // 4, columns // 8
    unit = 2 * 3 * rank * rank
    dense, rbasis, cbasis = dense_blocks[0], row_basis[0], col_basis[0]

    c2, c3, held, basis_held = pl.pallas_call(
        far_coefficients,
        out_shape=[
            pltpu.VMEM(shape, F32)
            for shape in ((quarter, rank), (quarter, rank), (users, columns // 2), (users, rank))
        ],
        in_specs=[ANY] * 2,
        out_specs=[VMEM] * 4,
        scratch_shapes=[
            pltpu.VMEM((columns // 2, rank), F32),
            pltpu.SemaphoreType.DMA((2, CHUNKS)),
        ],
        **settings(3 * users * columns * rank, users * columns, "far_coefficients"),
    )(*in_hbm([ratings, cbasis]))
    c2, c3 = swap(c2, 2), swap(c3, 3)
    c0, c1, near_above, dense_rest, held = pl.pallas_call(
        own_and_near,
        out_shape=[
            pltpu.VMEM(shape, F32)
            for shape in (
                (quarter, rank),
                (quarter, rank),
                (users // 2, columns),
                (users // 2, users),
                (users, columns),
            )
        ],
        in_specs=[VMEM, VMEM, ANY, ANY],
        out_specs=[VMEM] * 5,
        scratch_shapes=[
            pltpu.VMEM((columns // 2, rank), F32),
            pltpu.VMEM((users // 2, users), F32),
            pltpu.SemaphoreType.DMA((CHUNKS + 1,)),
            pltpu.SemaphoreType.DMA,
        ],
        **settings(3 * users * users * columns, users * users, "own_and_near"),
    )(*in_vmem([held, basis_held]), *in_hbm([ratings, dense]))
    c1 = swap(c1, 1)
    (near_below,) = run(
        near_field,
        [dense_rest, held],
        [(users // 2, columns)],
        "near_field",
        3 * users * users * columns,
    )
    coef = [c0, c1, c2, c3]
    a, rest = run(
        lift_leaves,
        [*coef, transfers],
        [(slim, rank)] * 2,
        "lift_leaves",
        unit * columns,
        scratch=[(quarter, rank)],
    )
    got_a, got_b = to_nodes(a, rest)
    leaf_fields = run(
        couple_leaves, [*coef, couplings], [(quarter, rank)] * 4, "couple_leaves", unit * 3 * columns
    )
    (ours,) = run(
        merge, [got_a, got_b], [(quarter, rank)], "merge_nodes", quarter * rank, after=leaf_fields
    )
    theirs = swap(ours, 1)
    leaf_fields = [leaf_fields[0]] + [swap(leaf_fields[j], j) for j in (1, 2, 3)]
    crown, parts = run(
        lift_nodes,
        [ours, theirs, transfers],
        [(slim, rank), (4 * slim, rank)],
        "lift_nodes",
        unit * 4 * slim,
    )
    (ours,) = run(merge, to_tops(crown), [(quarter, rank)], "merge_tops", quarter * rank)
    theirs = swap(ours, 1)
    node_fields = run(
        couple_nodes, [parts, couplings], [(slim, rank)] * 2, "couple_nodes", unit * 6 * slim
    )
    a, rest = run(
        top,
        [ours, theirs, couplings, transfers, *node_fields],
        [(slim, rank)] * 2,
        "top",
        unit * 5 * slim,
        after=leaf_fields[2:3],
    )
    (parent,) = run(
        merge_slices, to_nodes(a, rest), [(quarter, rank)], "merge_slices", quarter * rank
    )
    far_parent = swap(parent, 2)
    parents = [parent, swap(parent, 1)]

    def write(first, count, out):
        wide = count * quarter
        pieces = [x for j in range(first, first + count) for x in (leaf_fields[j], parents[j])]
        ins = in_vmem([near_above, near_below, rbasis, transfers, *pieces])
        return pl.pallas_call(
            functools.partial(finish, first),
            out_shape=pltpu.HBM((users, columns), F32),
            in_specs=[VMEM] * len(ins) + [ANY] * len(out),
            out_specs=ANY,
            scratch_shapes=[
                pltpu.VMEM((users, wide), F32),
                pltpu.VMEM((wide, rank), F32),
                pltpu.SemaphoreType.DMA((CHUNKS,)),
            ],
            input_output_aliases={len(ins): 0} if out else {},
            **settings(6 * users * rank * wide, users * wide, "finish_%d" % first),
        )(*ins, *out)

    out = write(0, 2, [])
    (relayed,) = run(
        relay, [far_parent], [(quarter, rank)], "relay", quarter * rank, after=in_hbm([out])
    )
    parents += [relayed, swap(relayed, 1)]
    out = write(2, 1, [out])
    return write(3, 1, [out])


def solution(mesh):
    placed = (
        P("leaf", "col"),
        P("leaf", None, None),
        P("leaf", None, None),
        P("leaf", None, None),
        P(),
        P(),
    )
    return jax.shard_map(
        local, mesh=mesh, in_specs=placed, out_specs=P("leaf", "col"), check_vma=False
    )
```

```python
import functools

import jax
import jax.numpy as jnp
from jax import lax
from jax.experimental import pallas as pl
from jax.experimental.pallas import tpu as pltpu
from jax.sharding import PartitionSpec as P


F32 = jnp.float32
HIGH = lax.Precision.HIGH
MIB = 1 << 20
VMEM = pl.BlockSpec(memory_space=pltpu.VMEM)
ANY = pl.BlockSpec(memory_space=pl.ANY)
CHUNKS = 4


def dot(a, b, ca, cb):
    return lax.dot_general(
        a, b, (((ca,), (cb,)), ((), ())), precision=HIGH, preferred_element_type=F32
    )


def in_vmem(arrays):
    return [pltpu.with_memory_space_constraint(x, pltpu.VMEM) for x in arrays]


def in_hbm(arrays):
    return [pltpu.with_memory_space_constraint(x, pltpu.HBM) for x in arrays]


def settings(flops, size, name):
    return dict(
        compiler_params=pltpu.CompilerParams(vmem_limit_bytes=24 * MIB),
        cost_estimate=pl.CostEstimate(flops=flops, bytes_accessed=4 * size, transcendentals=0),
        name=name,
    )


def run(body, ins, outs, name, flops, after=(), scratch=()):
    def kernel(*refs):
        body(*refs[: len(ins)], *refs[len(ins) + len(after) :])

    return pl.pallas_call(
        kernel,
        out_shape=[pltpu.VMEM(shape, F32) for shape in outs],
        in_specs=[VMEM] * len(ins) + [ANY] * len(after),
        out_specs=[VMEM] * len(outs),
        scratch_shapes=[pltpu.VMEM(shape, F32) for shape in scratch],
        **settings(flops, sum(x.size for x in ins), name),
    )(*in_vmem(ins), *after)


def place():
    leaf = lax.axis_index("leaf")
    return leaf // 16, leaf // 4 % 4, leaf % 4, leaf % 2


def mine(m, k):
    return k ^ (m & 2)


def span(index, count):
    return pl.ds(pl.multiple_of(index * count, count), count)


def offset(source, target):
    return (source - target + 4) % 4 - 1


def far_coefficients(x, basis, o2, o3, held, basis_held, whole, sems, rest_sem):
    _, m, k, _ = place()
    users, wide = x.shape[0], x.shape[1] // 2
    chunk = users // CHUNKS
    far = 1 - mine(m, k) // 2
    columns = span(far, wide)
    copies = []
    for i in range(CHUNKS):
        at = pl.ds(i * chunk, chunk)
        pair = (
            pltpu.make_async_copy(basis.at[at], basis_held.at[at], sems.at[0, i]),
            pltpu.make_async_copy(x.at[at, columns], held.at[at, columns], sems.at[1, i]),
        )
        for copy in pair:
            copy.start()
        copies.append(pair)
    near_columns = span(1 - far, wide)
    rest = pltpu.make_async_copy(x.at[:, near_columns], held.at[:, near_columns], rest_sem)
    rest.start()
    for i, pair in enumerate(copies):
        at = pl.ds(i * chunk, chunk)
        for copy in pair:
            copy.wait()
        term = dot(held[at, columns], basis_held[at, :], 0, 0)
        whole[...] = term if i == 0 else whole[...] + term
    for j, out in ((2, o2), (3, o3)):
        out[...] = whole[span((mine(m, k) ^ j) % 2, wide // 2), :]
    rest.wait()


def near_rows(dense, first, held, sems, x, out, meanwhile=None):
    count, chunk = len(sems), out.shape[0] // len(sems)
    copies = [
        pltpu.make_async_copy(
            dense.at[pl.ds(first + i * chunk, chunk)], held.at[pl.ds(i * chunk, chunk)], sems[i]
        )
        for i in range(count)
    ]
    for copy in copies:
        copy.start()
    if meanwhile is not None:
        meanwhile()
    for i, copy in enumerate(copies):
        at = pl.ds(i * chunk, chunk)
        copy.wait()
        out[at, :] = dot(held[at, :], x[...], 1, 0)


def own_and_near(held, basis_held, dense, o0, o1, out, whole, dense_held, sems):
    _, m, k, _ = place()
    wide = held.shape[1] // 2

    def own():
        whole[...] = dot(held[:, span(mine(m, k) // 2, wide)], basis_held[...], 0, 0)
        for j, piece in ((0, o0), (1, o1)):
            piece[...] = whole[span((mine(m, k) ^ j) % 2, wide // 2), :]

    near_rows(dense, 0, dense_held, [sems.at[i] for i in (0, 1)], held, out, own)


def near_field(dense, x, _, out, dense_held, sems):
    half = out.shape[0]
    near_rows(dense, half, dense_held, [sems.at[i] for i in (0, 1)], x, out)


def lift(level, digit, c0, c1, c2, c3, transfers, out):
    own = place()[digit]
    parts = (c0, c1, c2, c3)
    out[...] = sum(dot(c[...], transfers[level, own ^ j], 1, 0) for j, c in enumerate(parts))


def couple(level, digit, c0, c1, c2, c3, couplings, *fields):
    own = place()[digit]
    parts = (c0, c1, c2, c3)
    for target, out in enumerate(fields):
        at = own ^ target
        out[...] = sum(
            dot(parts[target ^ d][...], couplings[level, offset(at ^ d, at)], 1, 1) for d in (1, 2, 3)
        )


def turn(couplings, transfers, top_turned, node_turned, leaf_turned):
    _, m, _, _ = place()
    for i in range(3):
        top_turned[i] = couplings[2, i].T
    node_turned[...] = transfers[1, m].T
    for i in range(4):
        leaf_turned[i] = transfers[0, i].T


def descend(c1, c2, c3, top_turned, node_turned, leaf_turned, field, f0, f1, f2, f3, *outs):
    r, _, k, _ = place()
    parts = (c1, c2, c3)
    g = sum(dot(c[...], top_turned[offset(r ^ d, r)], 1, 0) for d, c in zip((1, 2, 3), parts))
    g = field[...] + dot(g, node_turned[...], 1, 0)
    for j, (f, out) in enumerate(zip((f0, f1, f2, f3), outs)):
        out[...] = f[...] + dot(g, leaf_turned[k ^ j], 1, 0)


def finish(first, near_above, near_below, row_basis, *rest):
    out, block, whole, sems = rest[-4:]
    _, m, k, _ = place()
    wide, step = whole.shape[0], rest[0].shape[0]
    if wide == step:
        whole[...] = rest[0][...]
        columns = span(mine(m, k) ^ first, wide)
    else:
        for j in (0, 1):
            whole[span((mine(m, k) ^ j) % 2, step), :] = rest[j][...]
        columns = span((mine(m, k) ^ first) // 2, wide)
    chunk = out.shape[0] // CHUNKS
    copies = []
    for i in range(CHUNKS):
        at = pl.ds(i * chunk, chunk)
        near = near_above if 2 * i < CHUNKS else near_below
        part = near[pl.ds(i * chunk % near.shape[0], chunk), columns]
        block[at, :] = part + dot(row_basis[at, :], whole[...], 1, 1)
        copy = pltpu.make_async_copy(block.at[at], out.at[at, columns], sems.at[i])
        copy.start()
        copies.append(copy)
    for copy in copies:
        copy.wait()


def swap(block, bits):
    return lax.ppermute(block, "leaf", [(i, i ^ bits) for i in range(lax.axis_size("leaf"))])


def local(ratings, dense_blocks, row_basis, col_basis, transfers, couplings):
    users, columns = ratings.shape
    rank = col_basis.shape[2]
    quarter = columns // 4
    unit = 2 * 3 * rank * rank
    dense, rbasis, cbasis = dense_blocks[0], row_basis[0], col_basis[0]

    c2, c3, held, basis_held = pl.pallas_call(
        far_coefficients,
        out_shape=[
            pltpu.VMEM(shape, F32)
            for shape in ((quarter, rank), (quarter, rank), (users, columns), (users, rank))
        ],
        in_specs=[ANY] * 2,
        out_specs=[VMEM] * 4,
        scratch_shapes=[
            pltpu.VMEM((columns // 2, rank), F32),
            pltpu.SemaphoreType.DMA((2, CHUNKS)),
            pltpu.SemaphoreType.DMA,
        ],
        **settings(3 * users * columns * rank, users * columns, "far_coefficients"),
    )(*in_hbm([ratings, cbasis]))
    c2, c3 = swap(c2, 2), swap(c3, 3)
    half_rows = (users // 2, columns)
    dense_half = [pltpu.VMEM((users // 2, users), F32), pltpu.SemaphoreType.DMA((2,))]
    c0, c1, near_above = pl.pallas_call(
        own_and_near,
        out_shape=[pltpu.VMEM(shape, F32) for shape in ((quarter, rank), (quarter, rank), half_rows)],
        in_specs=[VMEM, VMEM, ANY],
        out_specs=[VMEM] * 3,
        scratch_shapes=[pltpu.VMEM((columns // 2, rank), F32), *dense_half],
        **settings(3 * users * users * columns, users * users, "own_and_near"),
    )(*in_vmem([held, basis_held]), *in_hbm([dense]))
    c1 = swap(c1, 1)
    coef = [c0, c1, c2, c3]
    (lifted,) = run(
        functools.partial(lift, 0, 2),
        [*coef, transfers],
        [(quarter, rank)],
        "lift_leaves",
        unit * columns,
    )
    node_coef = [lifted] + [swap(lifted, bits) for bits in (4, 10, 14)]
    near_below = pl.pallas_call(
        near_field,
        out_shape=pltpu.VMEM(half_rows, F32),
        in_specs=[ANY, VMEM, ANY],
        out_specs=VMEM,
        scratch_shapes=dense_half,
        **settings(3 * users * users * columns, users * users, "near_field"),
    )(*in_hbm([dense]), *in_vmem([held]), lifted)
    leaf_fields = run(
        functools.partial(couple, 0, 2),
        [*coef, couplings],
        [(quarter, rank)] * 4,
        "couple_leaves",
        unit * 3 * columns,
    )
    turned = run(
        turn,
        [couplings, transfers],
        [(3, rank, rank), (rank, rank), (4, rank, rank)],
        "turn",
        unit * 8 * rank,
        after=[lifted],
    )
    (crown,) = run(
        functools.partial(lift, 1, 1),
        [*node_coef, transfers],
        [(quarter, rank)],
        "lift_nodes",
        unit * columns,
        after=[*leaf_fields, near_below, turned[1]],
    )
    top_coef = [swap(crown, bits) for bits in (16, 32, 48)]
    (node_field,) = run(
        functools.partial(couple, 1, 1),
        [*node_coef, couplings],
        [(quarter, rank)],
        "couple_nodes",
        unit * 3 * quarter,
    )
    g0, g1, g2, g3 = run(
        descend,
        [*top_coef, *turned, node_field, *leaf_fields],
        [(quarter, rank)] * 4,
        "descend",
        unit * 8 * quarter,
    )
    g2, g3, g1 = swap(g2, 2), swap(g3, 3), swap(g1, 1)

    def write(first, pieces, out):
        wide = len(pieces) * quarter
        return pl.pallas_call(
            functools.partial(finish, first),
            out_shape=pltpu.HBM((users, columns), F32),
            in_specs=[VMEM] * (3 + len(pieces)) + [ANY] * len(out),
            out_specs=ANY,
            scratch_shapes=[
                pltpu.VMEM((users, wide), F32),
                pltpu.VMEM((wide, rank), F32),
                pltpu.SemaphoreType.DMA((CHUNKS,)),
            ],
            input_output_aliases={3 + len(pieces): 0} if out else {},
            **settings(6 * users * rank * wide, users * wide, "finish_%d" % first),
        )(*in_vmem([near_above, near_below, rbasis, *pieces]), *out)

    out = write(0, [g0, g1], [])
    out = write(2, [g2], [out])
    return write(3, [g3], [out])


def solution(mesh):
    placed = (
        P("leaf", "col"),
        P("leaf", None, None),
        P("leaf", None, None),
        P("leaf", None, None),
        P(),
        P(),
    )
    return jax.shard_map(
        local, mesh=mesh, in_specs=placed, out_specs=P("leaf", "col"), check_vma=False
    )
```

```python
import functools

import jax
import jax.numpy as jnp
from jax import lax
from jax.experimental import pallas as pl
from jax.experimental.pallas import tpu as pltpu
from jax.sharding import PartitionSpec as P


F32 = jnp.float32
HIGH = lax.Precision.HIGH
MIB = 1 << 20
VMEM = pl.BlockSpec(memory_space=pltpu.VMEM)
ANY = pl.BlockSpec(memory_space=pl.ANY)
CHUNKS = 4


def dot(a, b, ca, cb):
    return lax.dot_general(
        a, b, (((ca,), (cb,)), ((), ())), precision=HIGH, preferred_element_type=F32
    )


def in_vmem(arrays):
    return [pltpu.with_memory_space_constraint(x, pltpu.VMEM) for x in arrays]


def in_hbm(arrays):
    return [pltpu.with_memory_space_constraint(x, pltpu.HBM) for x in arrays]


def settings(flops, size, name):
    return dict(
        compiler_params=pltpu.CompilerParams(vmem_limit_bytes=24 * MIB),
        cost_estimate=pl.CostEstimate(flops=flops, bytes_accessed=4 * size, transcendentals=0),
        name=name,
    )


def run(body, ins, outs, name, flops, after=(), scratch=()):
    def kernel(*refs):
        body(*refs[: len(ins)], *refs[len(ins) + len(after) :])

    return pl.pallas_call(
        kernel,
        out_shape=[pltpu.VMEM(shape, F32) for shape in outs],
        in_specs=[VMEM] * len(ins) + [ANY] * len(after),
        out_specs=[VMEM] * len(outs),
        scratch_shapes=[pltpu.VMEM(shape, F32) for shape in scratch],
        **settings(flops, sum(x.size for x in ins), name),
    )(*in_vmem(ins), *after)


def place():
    leaf = lax.axis_index("leaf")
    return leaf // 16, leaf // 4 % 4, leaf % 4, leaf % 2


def mine(m, k):
    return k ^ (m & 2)


def span(index, count):
    return pl.ds(pl.multiple_of(index * count, count), count)


def offset(source, target):
    return (source - target + 4) % 4 - 1


def far_coefficients(x, basis, o2, o3, held, basis_held, whole, sems, rest_sem):
    _, m, k, _ = place()
    users, wide = x.shape[0], x.shape[1] // 2
    chunk = users // CHUNKS
    far = 1 - mine(m, k) // 2
    columns = span(far, wide)
    copies = []
    for i in range(CHUNKS):
        at = pl.ds(i * chunk, chunk)
        pair = (
            pltpu.make_async_copy(basis.at[at], basis_held.at[at], sems.at[0, i]),
            pltpu.make_async_copy(x.at[at, columns], held.at[at, columns], sems.at[1, i]),
        )
        for copy in pair:
            copy.start()
        copies.append(pair)
    near_columns = span(1 - far, wide)
    rest = pltpu.make_async_copy(x.at[:, near_columns], held.at[:, near_columns], rest_sem)
    rest.start()
    for i, pair in enumerate(copies):
        at = pl.ds(i * chunk, chunk)
        for copy in pair:
            copy.wait()
        term = dot(held[at, columns], basis_held[at, :], 0, 0)
        whole[...] = term if i == 0 else whole[...] + term
    for j, out in ((2, o2), (3, o3)):
        out[...] = whole[span((mine(m, k) ^ j) % 2, wide // 2), :]
    rest.wait()


def near_rows(dense, first, held, sems, x, out, meanwhile=None):
    count, chunk = len(sems), out.shape[0] // len(sems)
    copies = [
        pltpu.make_async_copy(
            dense.at[pl.ds(first + i * chunk, chunk)], held.at[pl.ds(i * chunk, chunk)], sems[i]
        )
        for i in range(count)
    ]
    for copy in copies:
        copy.start()
    if meanwhile is not None:
        meanwhile()
    for i, copy in enumerate(copies):
        at = pl.ds(i * chunk, chunk)
        copy.wait()
        out[at, :] = dot(held[at, :], x[...], 1, 0)


def own_and_near(held, basis_held, dense, o0, o1, out, whole, dense_held, sems):
    _, m, k, _ = place()
    wide = held.shape[1] // 2

    def own():
        whole[...] = dot(held[:, span(mine(m, k) // 2, wide)], basis_held[...], 0, 0)
        for j, piece in ((0, o0), (1, o1)):
            piece[...] = whole[span((mine(m, k) ^ j) % 2, wide // 2), :]

    near_rows(dense, 0, dense_held, [sems.at[i] for i in (0, 1)], held, out, own)


def near_below(dense, x, _, out, dense_rest, dense_held, sems):
    count = out.shape[0]
    rest = pltpu.make_async_copy(
        dense.at[pl.ds(dense.shape[0] - count, count)], dense_rest, sems.at[2]
    )
    near_rows(dense, 2 * count, dense_held, [sems.at[i] for i in (0, 1)], x, out, rest.start)
    rest.wait()


def near_last(dense, x, out):
    out[...] = dot(dense[...], x[...], 1, 0)


def lift(level, digit, siblings, *refs):
    *parts, transfers, out = refs
    own = place()[digit]
    out[...] = sum(dot(c[...], transfers[level, own ^ j], 1, 0) for j, c in zip(siblings, parts))


def couple(level, digit, siblings, *refs):
    own = place()[digit]
    parts = dict(zip(siblings, refs))
    couplings, *fields = refs[len(siblings) :]
    for target, out in enumerate(fields):
        at = own ^ target
        out[...] = sum(
            dot(parts[target ^ d][...], couplings[level, offset(at ^ d, at)], 1, 1) for d in (1, 2, 3)
        )


def turn(couplings, transfers, top_turned, node_turned, leaf_turned):
    _, m, _, _ = place()
    for i in range(3):
        top_turned[i] = couplings[2, i].T
    node_turned[...] = transfers[1, m].T
    for i in range(4):
        leaf_turned[i] = transfers[0, i].T


def descend(c1, c2, c3, top_turned, node_turned, leaf_turned, field, f0, f1, f2, f3, *outs):
    r, _, k, _ = place()
    parts = (c1, c2, c3)
    g = sum(dot(c[...], top_turned[offset(r ^ d, r)], 1, 0) for d, c in zip((1, 2, 3), parts))
    g = field[...] + dot(g, node_turned[...], 1, 0)
    for j, (f, out) in enumerate(zip((f0, f1, f2, f3), outs)):
        out[...] = f[...] + dot(g, leaf_turned[k ^ j], 1, 0)


def finish(first, near_above, near_third, near_fourth, row_basis, *rest):
    out, block, whole, sems = rest[-4:]
    _, m, k, _ = place()
    wide, step = whole.shape[0], rest[0].shape[0]
    if wide == step:
        whole[...] = rest[0][...]
        columns = span(mine(m, k) ^ first, wide)
    else:
        for j in (0, 1):
            whole[span((mine(m, k) ^ j) % 2, step), :] = rest[j][...]
        columns = span((mine(m, k) ^ first) // 2, wide)
    chunk = out.shape[0] // CHUNKS
    copies = []
    for i in range(CHUNKS):
        at = pl.ds(i * chunk, chunk)
        near = (near_above, near_above, near_third, near_fourth)[i]
        part = near[pl.ds(i * chunk % near.shape[0], chunk), columns]
        block[at, :] = part + dot(row_basis[at, :], whole[...], 1, 1)
        copy = pltpu.make_async_copy(block.at[at], out.at[at, columns], sems.at[i])
        copy.start()
        copies.append(copy)
    for copy in copies:
        copy.wait()


def swap(block, bits):
    return lax.ppermute(block, "leaf", [(i, i ^ bits) for i in range(lax.axis_size("leaf"))])


def local(ratings, dense_blocks, row_basis, col_basis, transfers, couplings):
    users, columns = ratings.shape
    rank = col_basis.shape[2]
    quarter = columns // 4
    unit = 2 * 3 * rank * rank
    dense, rbasis, cbasis = dense_blocks[0], row_basis[0], col_basis[0]

    c2, c3, held, basis_held = pl.pallas_call(
        far_coefficients,
        out_shape=[
            pltpu.VMEM(shape, F32)
            for shape in ((quarter, rank), (quarter, rank), (users, columns), (users, rank))
        ],
        in_specs=[ANY] * 2,
        out_specs=[VMEM] * 4,
        scratch_shapes=[
            pltpu.VMEM((columns // 2, rank), F32),
            pltpu.SemaphoreType.DMA((2, CHUNKS)),
            pltpu.SemaphoreType.DMA,
        ],
        **settings(3 * users * columns * rank, users * columns, "far_coefficients"),
    )(*in_hbm([ratings, cbasis]))
    c2, c3 = swap(c2, 2), swap(c3, 3)
    half_rows = (users // 2, columns)
    dense_half = [pltpu.VMEM((users // 2, users), F32), pltpu.SemaphoreType.DMA((2,))]
    c0, c1, near_above = pl.pallas_call(
        own_and_near,
        out_shape=[pltpu.VMEM(shape, F32) for shape in ((quarter, rank), (quarter, rank), half_rows)],
        in_specs=[VMEM, VMEM, ANY],
        out_specs=[VMEM] * 3,
        scratch_shapes=[pltpu.VMEM((columns // 2, rank), F32), *dense_half],
        **settings(3 * users * users * columns, users * users, "own_and_near"),
    )(*in_vmem([held, basis_held]), *in_hbm([dense]))
    c1 = swap(c1, 1)
    coef = [c0, c1, c2, c3]
    (lifted,) = run(
        functools.partial(lift, 0, 2, range(4)),
        [*coef, transfers],
        [(quarter, rank)],
        "lift_leaves",
        unit * columns,
    )
    nodes = (0, 2, 3, 1)
    node_coef = [swap(lifted, (j << 2) | (j & 2)) if j else lifted for j in nodes]
    part_rows = (users // 4, columns)
    near_third, dense_rest = pl.pallas_call(
        near_below,
        out_shape=[pltpu.VMEM(part_rows, F32), pltpu.VMEM((users // 4, users), F32)],
        in_specs=[ANY, VMEM, ANY],
        out_specs=[VMEM] * 2,
        scratch_shapes=[pltpu.VMEM((users // 4, users), F32), pltpu.SemaphoreType.DMA((3,))],
        **settings(users * users * columns, users * users, "near_below"),
    )(*in_hbm([dense]), *in_vmem([held]), lifted)
    leaf_fields = run(
        functools.partial(couple, 0, 2, range(4)),
        [*coef, couplings],
        [(quarter, rank)] * 4,
        "couple_leaves",
        unit * 3 * columns,
    )
    turned = run(
        turn,
        [couplings, transfers],
        [(3, rank, rank), (rank, rank), (4, rank, rank)],
        "turn",
        unit * 8 * rank,
        after=[lifted],
    )
    (crown,) = run(
        functools.partial(lift, 1, 1, nodes),
        [*node_coef, transfers],
        [(quarter, rank)],
        "lift_nodes",
        unit * columns,
        after=[*leaf_fields, near_third, turned[1]],
    )
    top_coef = [swap(crown, bits) for bits in (16, 32, 48)]
    (node_field,) = run(
        functools.partial(couple, 1, 1, nodes),
        [*node_coef, couplings],
        [(quarter, rank)],
        "couple_nodes",
        unit * 3 * quarter,
    )
    g0, g1, g2, g3 = run(
        descend,
        [*top_coef, *turned, node_field, *leaf_fields],
        [(quarter, rank)] * 4,
        "descend",
        unit * 8 * quarter,
    )
    (near_fourth,) = run(
        near_last,
        [dense_rest, held],
        [part_rows],
        "near_last",
        3 * users * users * columns,
        after=[g0],
    )
    nears = [near_above, near_third, near_fourth]
    g2, g3, g1 = swap(g2, 2), swap(g3, 3), swap(g1, 1)

    def write(first, pieces, out):
        wide = len(pieces) * quarter
        return pl.pallas_call(
            functools.partial(finish, first),
            out_shape=pltpu.HBM((users, columns), F32),
            in_specs=[VMEM] * (4 + len(pieces)) + [ANY] * len(out),
            out_specs=ANY,
            scratch_shapes=[
                pltpu.VMEM((users, wide), F32),
                pltpu.VMEM((wide, rank), F32),
                pltpu.SemaphoreType.DMA((CHUNKS,)),
            ],
            input_output_aliases={4 + len(pieces): 0} if out else {},
            **settings(6 * users * rank * wide, users * wide, "finish_%d" % first),
        )(*in_vmem([*nears, rbasis, *pieces]), *out)

    out = write(0, [g0, g1], [])
    out = write(2, [g2], [out])
    return write(3, [g3], [out])


def solution(mesh):
    placed = (
        P("leaf", "col"),
        P("leaf", None, None),
        P("leaf", None, None),
        P("leaf", None, None),
        P(),
        P(),
    )
    return jax.shard_map(
        local, mesh=mesh, in_specs=placed, out_specs=P("leaf", "col"), check_vma=False
    )
```

```python
import functools

import jax
import jax.numpy as jnp
from jax import lax
from jax.experimental import pallas as pl
from jax.experimental.pallas import tpu as pltpu
from jax.sharding import PartitionSpec as P


F32 = jnp.float32
HIGH = lax.Precision.HIGH
MIB = 1 << 20
VMEM = pl.BlockSpec(memory_space=pltpu.VMEM)
ANY = pl.BlockSpec(memory_space=pl.ANY)
CHUNKS = 4


def dot(a, b, ca, cb):
    return lax.dot_general(
        a, b, (((ca,), (cb,)), ((), ())), precision=HIGH, preferred_element_type=F32
    )


def in_vmem(arrays):
    return [pltpu.with_memory_space_constraint(x, pltpu.VMEM) for x in arrays]


def in_hbm(arrays):
    return [pltpu.with_memory_space_constraint(x, pltpu.HBM) for x in arrays]


def settings(flops, size, name):
    return dict(
        compiler_params=pltpu.CompilerParams(vmem_limit_bytes=24 * MIB),
        cost_estimate=pl.CostEstimate(flops=flops, bytes_accessed=4 * size, transcendentals=0),
        name=name,
    )


def run(body, ins, outs, name, flops, after=(), scratch=()):
    def kernel(*refs):
        body(*refs[: len(ins)], *refs[len(ins) + len(after) :])

    return pl.pallas_call(
        kernel,
        out_shape=[pltpu.VMEM(shape, F32) for shape in outs],
        in_specs=[VMEM] * len(ins) + [ANY] * len(after),
        out_specs=[VMEM] * len(outs),
        scratch_shapes=[pltpu.VMEM(shape, F32) for shape in scratch],
        **settings(flops, sum(x.size for x in ins), name),
    )(*in_vmem(ins), *after)


def place():
    leaf = lax.axis_index("leaf")
    return leaf // 16, leaf // 4 % 4, leaf % 4, leaf % 2


def mine(m, k):
    return k ^ (m & 2)


def span(index, count):
    return pl.ds(pl.multiple_of(index * count, count), count)


def offset(source, target):
    return (source - target + 4) % 4 - 1


def far_coefficients(x, basis, o2, o3, held, basis_held, whole, sems, rest_sem):
    _, m, k, _ = place()
    users, wide = x.shape[0], x.shape[1] // 2
    chunk = users // CHUNKS
    far = 1 - mine(m, k) // 2
    columns = span(far, wide)
    copies = []
    for i in range(CHUNKS):
        at = pl.ds(i * chunk, chunk)
        pair = (
            pltpu.make_async_copy(basis.at[at], basis_held.at[at], sems.at[0, i]),
            pltpu.make_async_copy(x.at[at, columns], held.at[at, columns], sems.at[1, i]),
        )
        for copy in pair:
            copy.start()
        copies.append(pair)
    near_columns = span(1 - far, wide)
    rest = pltpu.make_async_copy(x.at[:, near_columns], held.at[:, near_columns], rest_sem)
    rest.start()
    for i, pair in enumerate(copies):
        at = pl.ds(i * chunk, chunk)
        for copy in pair:
            copy.wait()
        term = dot(held[at, columns], basis_held[at, :], 0, 0)
        whole[...] = term if i == 0 else whole[...] + term
    for j, out in ((2, o2), (3, o3)):
        out[...] = whole[span((mine(m, k) ^ j) % 2, wide // 2), :]
    rest.wait()


def near_rows(dense, first, held, sems, x, out, meanwhile=None):
    count, chunk = len(sems), out.shape[0] // len(sems)
    copies = [
        pltpu.make_async_copy(
            dense.at[pl.ds(first + i * chunk, chunk)], held.at[pl.ds(i * chunk, chunk)], sems[i]
        )
        for i in range(count)
    ]
    for copy in copies:
        copy.start()
    if meanwhile is not None:
        meanwhile()
    for i, copy in enumerate(copies):
        at = pl.ds(i * chunk, chunk)
        copy.wait()
        out[at, :] = dot(held[at, :], x[...], 1, 0)


def own_and_near(held, basis_held, dense, o0, o1, out, whole, dense_held, sems):
    _, m, k, _ = place()
    wide = held.shape[1] // 2

    def own():
        whole[...] = dot(held[:, span(mine(m, k) // 2, wide)], basis_held[...], 0, 0)
        for j, piece in ((0, o0), (1, o1)):
            piece[...] = whole[span((mine(m, k) ^ j) % 2, wide // 2), :]

    near_rows(dense, 0, dense_held, [sems.at[i] for i in (0, 1)], held, out, own)


def near_below(dense, x, _, out, dense_rest, dense_held, sems):
    count = out.shape[0]
    rest = pltpu.make_async_copy(
        dense.at[pl.ds(dense.shape[0] - count, count)], dense_rest, sems.at[2]
    )
    near_rows(dense, 2 * count, dense_held, [sems.at[i] for i in (0, 1)], x, out, rest.start)
    rest.wait()


def near_last(dense, x, out):
    out[...] = dot(dense[...], x[...], 1, 0)


def lift(level, digit, siblings, *refs):
    *parts, transfers, out = refs
    own = place()[digit]
    out[...] = sum(dot(c[...], transfers[level, own ^ j], 1, 0) for j, c in zip(siblings, parts))


def couple(level, digit, siblings, *refs):
    own = place()[digit]
    parts = dict(zip(siblings, refs))
    couplings, *fields = refs[len(siblings) :]
    for target, out in enumerate(fields):
        at = own ^ target
        out[...] = sum(
            dot(parts[target ^ d][...], couplings[level, offset(at ^ d, at)], 1, 1) for d in (1, 2, 3)
        )


def turn(couplings, transfers, top_turned, node_turned, leaf_turned):
    _, m, _, _ = place()
    for i in range(3):
        top_turned[i] = couplings[2, i].T
    node_turned[...] = transfers[1, m].T
    for i in range(4):
        leaf_turned[i] = transfers[0, i].T


def descend(c1, c3, c2, top_turned, node_turned, leaf_turned, field, f0, f1, f2, f3, *outs):
    r, _, k, _ = place()
    parts = (c1, c2, c3)
    g = sum(dot(c[...], top_turned[offset(r ^ d, r)], 1, 0) for d, c in zip((1, 2, 3), parts))
    g = field[...] + dot(g, node_turned[...], 1, 0)
    for j, (f, out) in enumerate(zip((f0, f1, f2, f3), outs)):
        out[...] = f[...] + dot(g, leaf_turned[k ^ j], 1, 0)


def finish(first, near_above, near_third, near_fourth, row_basis, *rest):
    out, block, whole, sems = rest[-4:]
    _, m, k, _ = place()
    wide, step = whole.shape[0], rest[0].shape[0]
    if wide == step:
        whole[...] = rest[0][...]
        columns = span(mine(m, k) ^ first, wide)
    else:
        for j in (0, 1):
            whole[span((mine(m, k) ^ j) % 2, step), :] = rest[j][...]
        columns = span((mine(m, k) ^ first) // 2, wide)
    chunk = out.shape[0] // CHUNKS
    copies = []
    for i in range(CHUNKS):
        at = pl.ds(i * chunk, chunk)
        near = (near_above, near_above, near_third, near_fourth)[i]
        part = near[pl.ds(i * chunk % near.shape[0], chunk), columns]
        block[at, :] = part + dot(row_basis[at, :], whole[...], 1, 1)
        copy = pltpu.make_async_copy(block.at[at], out.at[at, columns], sems.at[i])
        copy.start()
        copies.append(copy)
    for copy in copies:
        copy.wait()


def swap(block, bits):
    return lax.ppermute(block, "leaf", [(i, i ^ bits) for i in range(lax.axis_size("leaf"))])


def local(ratings, dense_blocks, row_basis, col_basis, transfers, couplings):
    users, columns = ratings.shape
    rank = col_basis.shape[2]
    quarter = columns // 4
    unit = 2 * 3 * rank * rank
    dense, rbasis, cbasis = dense_blocks[0], row_basis[0], col_basis[0]

    c2, c3, held, basis_held = pl.pallas_call(
        far_coefficients,
        out_shape=[
            pltpu.VMEM(shape, F32)
            for shape in ((quarter, rank), (quarter, rank), (users, columns), (users, rank))
        ],
        in_specs=[ANY] * 2,
        out_specs=[VMEM] * 4,
        scratch_shapes=[
            pltpu.VMEM((columns // 2, rank), F32),
            pltpu.SemaphoreType.DMA((2, CHUNKS)),
            pltpu.SemaphoreType.DMA,
        ],
        **settings(3 * users * columns * rank, users * columns, "far_coefficients"),
    )(*in_hbm([ratings, cbasis]))
    c2, c3 = swap(c2, 2), swap(c3, 3)
    half_rows = (users // 2, columns)
    dense_half = [pltpu.VMEM((users // 2, users), F32), pltpu.SemaphoreType.DMA((2,))]
    c0, c1, near_above = pl.pallas_call(
        own_and_near,
        out_shape=[pltpu.VMEM(shape, F32) for shape in ((quarter, rank), (quarter, rank), half_rows)],
        in_specs=[VMEM, VMEM, ANY],
        out_specs=[VMEM] * 3,
        scratch_shapes=[pltpu.VMEM((columns // 2, rank), F32), *dense_half],
        **settings(3 * users * users * columns, users * users, "own_and_near"),
    )(*in_vmem([held, basis_held]), *in_hbm([dense]))
    c1 = swap(c1, 1)
    coef = [c0, c1, c2, c3]
    (lifted,) = run(
        functools.partial(lift, 0, 2, range(4)),
        [*coef, transfers],
        [(quarter, rank)],
        "lift_leaves",
        unit * columns,
    )
    nodes = (0, 2, 3, 1)
    node_coef = [swap(lifted, (j << 2) | (j & 2)) if j else lifted for j in nodes]
    part_rows = (users // 4, columns)
    near_third, dense_rest = pl.pallas_call(
        near_below,
        out_shape=[pltpu.VMEM(part_rows, F32), pltpu.VMEM((users // 4, users), F32)],
        in_specs=[ANY, VMEM, ANY],
        out_specs=[VMEM] * 2,
        scratch_shapes=[pltpu.VMEM((users // 4, users), F32), pltpu.SemaphoreType.DMA((3,))],
        **settings(users * users * columns, users * users, "near_below"),
    )(*in_hbm([dense]), *in_vmem([held]), lifted)
    leaf_fields = run(
        functools.partial(couple, 0, 2, range(4)),
        [*coef, couplings],
        [(quarter, rank)] * 4,
        "couple_leaves",
        unit * 3 * columns,
    )
    turned = run(
        turn,
        [couplings, transfers],
        [(3, rank, rank), (rank, rank), (4, rank, rank)],
        "turn",
        unit * 8 * rank,
        after=[lifted],
    )
    (crown,) = run(
        functools.partial(lift, 1, 1, nodes),
        [*node_coef, transfers],
        [(quarter, rank)],
        "lift_nodes",
        unit * columns,
        after=[*leaf_fields, near_third, turned[1]],
    )
    top_coef = [swap(crown, bits) for bits in (16, 48, 32)]
    (node_field,) = run(
        functools.partial(couple, 1, 1, nodes),
        [*node_coef, couplings],
        [(quarter, rank)],
        "couple_nodes",
        unit * 3 * quarter,
    )
    g0, g1, g2, g3 = run(
        descend,
        [*top_coef, *turned, node_field, *leaf_fields],
        [(quarter, rank)] * 4,
        "descend",
        unit * 8 * quarter,
    )
    (near_fourth,) = run(
        near_last,
        [dense_rest, held],
        [part_rows],
        "near_last",
        3 * users * users * columns,
        after=[g0],
    )
    nears = [near_above, near_third, near_fourth]
    g2, g3, g1 = swap(g2, 2), swap(g3, 3), swap(g1, 1)

    def write(first, pieces, out):
        wide = len(pieces) * quarter
        return pl.pallas_call(
            functools.partial(finish, first),
            out_shape=pltpu.HBM((users, columns), F32),
            in_specs=[VMEM] * (4 + len(pieces)) + [ANY] * len(out),
            out_specs=ANY,
            scratch_shapes=[
                pltpu.VMEM((users, wide), F32),
                pltpu.VMEM((wide, rank), F32),
                pltpu.SemaphoreType.DMA((CHUNKS,)),
            ],
            input_output_aliases={4 + len(pieces): 0} if out else {},
            **settings(6 * users * rank * wide, users * wide, "finish_%d" % first),
        )(*in_vmem([*nears, rbasis, *pieces]), *out)

    out = write(0, [g0, g1], [])
    return write(2, [g2, g3], [out])


def solution(mesh):
    placed = (
        P("leaf", "col"),
        P("leaf", None, None),
        P("leaf", None, None),
        P("leaf", None, None),
        P(),
        P(),
    )
    return jax.shard_map(
        local, mesh=mesh, in_specs=placed, out_specs=P("leaf", "col"), check_vma=False
    )
```

```python
import functools

import jax
import jax.numpy as jnp
from jax import lax
from jax.experimental import pallas as pl
from jax.experimental.pallas import tpu as pltpu
from jax.sharding import PartitionSpec as P


F32 = jnp.float32
HIGH = lax.Precision.HIGH
MIB = 1 << 20
VMEM = pl.BlockSpec(memory_space=pltpu.VMEM)
ANY = pl.BlockSpec(memory_space=pl.ANY)
CHUNKS = 4


def dot(a, b, ca, cb):
    return lax.dot_general(
        a, b, (((ca,), (cb,)), ((), ())), precision=HIGH, preferred_element_type=F32
    )


def in_vmem(arrays):
    return [pltpu.with_memory_space_constraint(x, pltpu.VMEM) for x in arrays]


def in_hbm(arrays):
    return [pltpu.with_memory_space_constraint(x, pltpu.HBM) for x in arrays]


def settings(flops, size, name):
    return dict(
        compiler_params=pltpu.CompilerParams(vmem_limit_bytes=24 * MIB),
        cost_estimate=pl.CostEstimate(flops=flops, bytes_accessed=4 * size, transcendentals=0),
        name=name,
    )


def run(body, ins, outs, name, flops, after=(), scratch=()):
    def kernel(*refs):
        body(*refs[: len(ins)], *refs[len(ins) + len(after) :])

    return pl.pallas_call(
        kernel,
        out_shape=[pltpu.VMEM(shape, F32) for shape in outs],
        in_specs=[VMEM] * len(ins) + [ANY] * len(after),
        out_specs=[VMEM] * len(outs),
        scratch_shapes=[pltpu.VMEM(shape, F32) for shape in scratch],
        **settings(flops, sum(x.size for x in ins), name),
    )(*in_vmem(ins), *after)


def place():
    leaf = lax.axis_index("leaf")
    return leaf // 16, leaf // 4 % 4, leaf % 4, leaf % 2


def mine(m, k):
    return k ^ (m & 2)


def span(index, count):
    return pl.ds(pl.multiple_of(index * count, count), count)


def offset(source, target):
    return (source - target + 4) % 4 - 1


def far_coefficients(x, basis, o2, o3, held, basis_held, whole, sems, rest_sem):
    _, m, k, _ = place()
    users, wide = x.shape[0], x.shape[1] // 2
    chunk = users // CHUNKS
    far = 1 - mine(m, k) // 2
    columns = span(far, wide)
    copies = []
    for i in range(CHUNKS):
        at = pl.ds(i * chunk, chunk)
        pair = (
            pltpu.make_async_copy(basis.at[at], basis_held.at[at], sems.at[0, i]),
            pltpu.make_async_copy(x.at[at, columns], held.at[at, columns], sems.at[1, i]),
        )
        for copy in pair:
            copy.start()
        copies.append(pair)
    near_columns = span(1 - far, wide)
    rest = pltpu.make_async_copy(x.at[:, near_columns], held.at[:, near_columns], rest_sem)
    rest.start()
    for i, pair in enumerate(copies):
        at = pl.ds(i * chunk, chunk)
        for copy in pair:
            copy.wait()
        term = dot(held[at, columns], basis_held[at, :], 0, 0)
        whole[...] = term if i == 0 else whole[...] + term
    for j, out in ((2, o2), (3, o3)):
        out[...] = whole[span((mine(m, k) ^ j) % 2, wide // 2), :]
    rest.wait()


def near_rows(dense, first, held, sems, x, out, meanwhile=None):
    count, chunk = len(sems), out.shape[0] // len(sems)
    copies = [
        pltpu.make_async_copy(
            dense.at[pl.ds(first + i * chunk, chunk)], held.at[pl.ds(i * chunk, chunk)], sems[i]
        )
        for i in range(count)
    ]
    for copy in copies:
        copy.start()
    if meanwhile is not None:
        meanwhile()
    for i, copy in enumerate(copies):
        at = pl.ds(i * chunk, chunk)
        copy.wait()
        out[at, :] = dot(held[at, :], x[...], 1, 0)


def own_and_near(held, basis_held, dense, o0, o1, out, whole, dense_held, sems):
    _, m, k, _ = place()
    wide = held.shape[1] // 2

    def own():
        whole[...] = dot(held[:, span(mine(m, k) // 2, wide)], basis_held[...], 0, 0)
        for j, piece in ((0, o0), (1, o1)):
            piece[...] = whole[span((mine(m, k) ^ j) % 2, wide // 2), :]

    near_rows(dense, 0, dense_held, [sems.at[i] for i in (0, 1)], held, out, own)


def near_below(dense, x, _, out, dense_rest, dense_held, sems):
    count = out.shape[0]
    rest = pltpu.make_async_copy(
        dense.at[pl.ds(dense.shape[0] - count, count)], dense_rest, sems.at[2]
    )
    near_rows(dense, 2 * count, dense_held, [sems.at[i] for i in (0, 1)], x, out, rest.start)
    rest.wait()


def near_last(dense, x, out):
    out[...] = dot(dense[...], x[...], 1, 0)


def lift(level, digit, siblings, *refs):
    *parts, transfers, out = refs
    own = place()[digit]
    out[...] = sum(dot(c[...], transfers[level, own ^ j], 1, 0) for j, c in zip(siblings, parts))


def couple(level, digit, siblings, *refs):
    own = place()[digit]
    parts = dict(zip(siblings, refs))
    couplings, *fields = refs[len(siblings) :]
    for target, out in enumerate(fields):
        at = own ^ target
        out[...] = sum(
            dot(parts[target ^ d][...], couplings[level, offset(at ^ d, at)], 1, 1) for d in (1, 2, 3)
        )


def turn(couplings, transfers, top_turned, node_turned, leaf_turned):
    _, m, _, _ = place()
    for i in range(3):
        top_turned[i] = couplings[2, i].T
    node_turned[...] = transfers[1, m].T
    for i in range(4):
        leaf_turned[i] = transfers[0, i].T


def descend(c2, c3, c1, top_turned, node_turned, field, out):
    r = place()[0]
    g = sum(
        dot(c[...], top_turned[offset(r ^ d, r)], 1, 0) for d, c in zip((2, 3, 1), (c2, c3, c1))
    )
    out[...] = field[...] + dot(g, node_turned[...], 1, 0)


def relay(block, out):
    out[...] = block[...]


def finish(
    first, near_above, near_third, near_fourth, row_basis, leaf_turned, f0, g0, f1, g1, *rest
):
    out, block, whole, sems = rest[-4:]
    _, m, k, _ = place()
    wide, step = whole.shape[0], g0.shape[0]
    for j, (field, parent) in enumerate(((f0, g0), (f1, g1))):
        at = span((mine(m, k) ^ j) % 2, step)
        whole[at, :] = field[...] + dot(parent[...], leaf_turned[k], 1, 0)
    columns = span((mine(m, k) ^ first) // 2, wide)
    chunk = out.shape[0] // CHUNKS
    copies = []
    for i in range(CHUNKS):
        at = pl.ds(i * chunk, chunk)
        near = (near_above, near_above, near_third, near_fourth)[i]
        part = near[pl.ds(i * chunk % near.shape[0], chunk), columns]
        block[at, :] = part + dot(row_basis[at, :], whole[...], 1, 1)
        copy = pltpu.make_async_copy(block.at[at], out.at[at, columns], sems.at[i])
        copy.start()
        copies.append(copy)
    for copy in copies:
        copy.wait()


def swap(block, bits):
    return lax.ppermute(block, "leaf", [(i, i ^ bits) for i in range(lax.axis_size("leaf"))])


def local(ratings, dense_blocks, row_basis, col_basis, transfers, couplings):
    users, columns = ratings.shape
    rank = col_basis.shape[2]
    quarter = columns // 4
    unit = 2 * 3 * rank * rank
    dense, rbasis, cbasis = dense_blocks[0], row_basis[0], col_basis[0]

    c2, c3, held, basis_held = pl.pallas_call(
        far_coefficients,
        out_shape=[
            pltpu.VMEM(shape, F32)
            for shape in ((quarter, rank), (quarter, rank), (users, columns), (users, rank))
        ],
        in_specs=[ANY] * 2,
        out_specs=[VMEM] * 4,
        scratch_shapes=[
            pltpu.VMEM((columns // 2, rank), F32),
            pltpu.SemaphoreType.DMA((2, CHUNKS)),
            pltpu.SemaphoreType.DMA,
        ],
        **settings(3 * users * columns * rank, users * columns, "far_coefficients"),
    )(*in_hbm([ratings, cbasis]))
    c2, c3 = swap(c2, 2), swap(c3, 3)
    half_rows = (users // 2, columns)
    dense_half = [pltpu.VMEM((users // 2, users), F32), pltpu.SemaphoreType.DMA((2,))]
    c0, c1, near_above = pl.pallas_call(
        own_and_near,
        out_shape=[pltpu.VMEM(shape, F32) for shape in ((quarter, rank), (quarter, rank), half_rows)],
        in_specs=[VMEM, VMEM, ANY],
        out_specs=[VMEM] * 3,
        scratch_shapes=[pltpu.VMEM((columns // 2, rank), F32), *dense_half],
        **settings(3 * users * users * columns, users * users, "own_and_near"),
    )(*in_vmem([held, basis_held]), *in_hbm([dense]))
    c1 = swap(c1, 1)
    leaves, coef = (0, 2, 3, 1), [c0, c2, c3, c1]
    (lifted,) = run(
        functools.partial(lift, 0, 2, leaves),
        [*coef, transfers],
        [(quarter, rank)],
        "lift_leaves",
        unit * columns,
    )
    nodes = (0, 1, 3, 2)
    node_coef = [swap(lifted, (j << 2) | (j & 2)) if j else lifted for j in nodes]
    part_rows = (users // 4, columns)
    near_third, dense_rest = pl.pallas_call(
        near_below,
        out_shape=[pltpu.VMEM(part_rows, F32), pltpu.VMEM((users // 4, users), F32)],
        in_specs=[ANY, VMEM, ANY],
        out_specs=[VMEM] * 2,
        scratch_shapes=[pltpu.VMEM((users // 4, users), F32), pltpu.SemaphoreType.DMA((3,))],
        **settings(users * users * columns, users * users, "near_below"),
    )(*in_hbm([dense]), *in_vmem([held]), lifted)
    leaf_fields = run(
        functools.partial(couple, 0, 2, leaves),
        [*coef, couplings],
        [(quarter, rank)] * 4,
        "couple_leaves",
        unit * 3 * columns,
    )
    turned = run(
        turn,
        [couplings, transfers],
        [(3, rank, rank), (rank, rank), (4, rank, rank)],
        "turn",
        unit * 8 * rank,
        after=[lifted],
    )
    (crown,) = run(
        functools.partial(lift, 1, 1, nodes),
        [*node_coef, transfers],
        [(quarter, rank)],
        "lift_nodes",
        unit * columns,
        after=[*leaf_fields, near_third, turned[1]],
    )
    top_coef = [swap(crown, bits) for bits in (32, 48, 16)]
    (node_field,) = run(
        functools.partial(couple, 1, 1, nodes),
        [*node_coef, couplings],
        [(quarter, rank)],
        "couple_nodes",
        unit * 3 * quarter,
    )
    fields = [leaf_fields[0]] + [swap(leaf_fields[j], j) for j in (1, 2, 3)]
    (parent,) = run(
        descend,
        [*top_coef, *turned[:2], node_field],
        [(quarter, rank)],
        "descend",
        unit * 4 * quarter,
        after=fields[2:3],
    )
    far_parent, core_parent = swap(parent, 2), swap(parent, 1)
    (near_fourth,) = run(
        near_last,
        [dense_rest, held],
        [part_rows],
        "near_last",
        3 * users * users * columns,
        after=[parent],
    )
    nears = [near_above, near_third, near_fourth]

    def write(first, pieces, out):
        ins = in_vmem([*nears, rbasis, turned[2], *pieces])
        return pl.pallas_call(
            functools.partial(finish, first),
            out_shape=pltpu.HBM((users, columns), F32),
            in_specs=[VMEM] * len(ins) + [ANY] * len(out),
            out_specs=ANY,
            scratch_shapes=[
                pltpu.VMEM((users, columns // 2), F32),
                pltpu.VMEM((columns // 2, rank), F32),
                pltpu.SemaphoreType.DMA((CHUNKS,)),
            ],
            input_output_aliases={len(ins): 0} if out else {},
            **settings(3 * users * rank * columns, users * columns, "finish_%d" % first),
        )(*ins, *out)

    out = write(0, [fields[0], parent, fields[1], core_parent], [])
    (far_parent,) = run(
        relay, [far_parent], [(quarter, rank)], "relay", quarter * rank, after=in_hbm([out])
    )
    return write(2, [fields[2], far_parent, fields[3], swap(far_parent, 1)], [out])


def solution(mesh):
    placed = (
        P("leaf", "col"),
        P("leaf", None, None),
        P("leaf", None, None),
        P("leaf", None, None),
        P(),
        P(),
    )
    return jax.shard_map(
        local, mesh=mesh, in_specs=placed, out_specs=P("leaf", "col"), check_vma=False
    )
```

```python
import functools

import jax
import jax.numpy as jnp
from jax import lax
from jax.experimental import pallas as pl
from jax.experimental.pallas import tpu as pltpu
from jax.sharding import PartitionSpec as P


F32 = jnp.float32
HIGH = lax.Precision.HIGH
MIB = 1 << 20
VMEM = pl.BlockSpec(memory_space=pltpu.VMEM)
ANY = pl.BlockSpec(memory_space=pl.ANY)
CHUNKS = 4


def dot(a, b, ca, cb):
    return lax.dot_general(
        a, b, (((ca,), (cb,)), ((), ())), precision=HIGH, preferred_element_type=F32
    )


def in_vmem(arrays):
    return [pltpu.with_memory_space_constraint(x, pltpu.VMEM) for x in arrays]


def in_hbm(arrays):
    return [pltpu.with_memory_space_constraint(x, pltpu.HBM) for x in arrays]


def settings(flops, size, name):
    return dict(
        compiler_params=pltpu.CompilerParams(vmem_limit_bytes=24 * MIB),
        cost_estimate=pl.CostEstimate(flops=flops, bytes_accessed=4 * size, transcendentals=0),
        name=name,
    )


def run(body, ins, outs, name, flops, after=(), scratch=()):
    def kernel(*refs):
        body(*refs[: len(ins)], *refs[len(ins) + len(after) :])

    return pl.pallas_call(
        kernel,
        out_shape=[pltpu.VMEM(shape, F32) for shape in outs],
        in_specs=[VMEM] * len(ins) + [ANY] * len(after),
        out_specs=[VMEM] * len(outs),
        scratch_shapes=[pltpu.VMEM(shape, F32) for shape in scratch],
        **settings(flops, sum(x.size for x in ins), name),
    )(*in_vmem(ins), *after)


def place():
    leaf = lax.axis_index("leaf")
    return leaf // 16, leaf // 4 % 4, leaf % 4, leaf % 2


def mine(m, k):
    return k ^ (m & 2)


def span(index, count):
    return pl.ds(pl.multiple_of(index * count, count), count)


def offset(source, target):
    return (source - target + 4) % 4 - 1


def far_coefficients(x, basis, o2, o3, held, basis_held, whole, sems, rest_sem):
    _, m, k, _ = place()
    users, wide = x.shape[0], x.shape[1] // 2
    chunk = users // CHUNKS
    far = 1 - mine(m, k) // 2
    columns = span(far, wide)
    copies = []
    for i in range(CHUNKS):
        at = pl.ds(i * chunk, chunk)
        pair = (
            pltpu.make_async_copy(basis.at[at], basis_held.at[at], sems.at[0, i]),
            pltpu.make_async_copy(x.at[at, columns], held.at[at, columns], sems.at[1, i]),
        )
        for copy in pair:
            copy.start()
        copies.append(pair)
    near_columns = span(1 - far, wide)
    rest = pltpu.make_async_copy(x.at[:, near_columns], held.at[:, near_columns], rest_sem)
    rest.start()
    for i, pair in enumerate(copies):
        at = pl.ds(i * chunk, chunk)
        for copy in pair:
            copy.wait()
        term = dot(held[at, columns], basis_held[at, :], 0, 0)
        whole[...] = term if i == 0 else whole[...] + term
    for j, out in ((2, o2), (3, o3)):
        out[...] = whole[span((mine(m, k) ^ j) % 2, wide // 2), :]
    rest.wait()


def near_rows(dense, first, held, sems, x, out, meanwhile=None):
    count, chunk = len(sems), out.shape[0] // len(sems)
    copies = [
        pltpu.make_async_copy(
            dense.at[pl.ds(first + i * chunk, chunk)], held.at[pl.ds(i * chunk, chunk)], sems[i]
        )
        for i in range(count)
    ]
    for copy in copies:
        copy.start()
    if meanwhile is not None:
        meanwhile()
    for i, copy in enumerate(copies):
        at = pl.ds(i * chunk, chunk)
        copy.wait()
        out[at, :] = dot(held[at, :], x[...], 1, 0)


def own_and_near(held, basis_held, dense, o0, o1, out, whole, dense_held, sems):
    _, m, k, _ = place()
    wide = held.shape[1] // 2

    def own():
        whole[...] = dot(held[:, span(mine(m, k) // 2, wide)], basis_held[...], 0, 0)
        for j, piece in ((0, o0), (1, o1)):
            piece[...] = whole[span((mine(m, k) ^ j) % 2, wide // 2), :]

    near_rows(dense, 0, dense_held, [sems.at[i] for i in (0, 1)], held, out, own)


def near_below(dense, x, _, out, dense_rest, dense_held, sems):
    count = out.shape[0]
    rest = pltpu.make_async_copy(
        dense.at[pl.ds(dense.shape[0] - count, count)], dense_rest, sems.at[2]
    )
    near_rows(dense, 2 * count, dense_held, [sems.at[i] for i in (0, 1)], x, out, rest.start)
    rest.wait()


def near_last(dense, x, out):
    out[...] = dot(dense[...], x[...], 1, 0)


def lift(level, digit, siblings, *refs):
    *parts, transfers, out = refs
    own = place()[digit]
    out[...] = sum(dot(c[...], transfers[level, own ^ j], 1, 0) for j, c in zip(siblings, parts))


def couple(level, digit, siblings, *refs):
    own = place()[digit]
    parts = dict(zip(siblings, refs))
    couplings, *fields = refs[len(siblings) :]
    for target, out in enumerate(fields):
        at = own ^ target
        out[...] = sum(
            dot(parts[target ^ d][...], couplings[level, offset(at ^ d, at)], 1, 1) for d in (1, 2, 3)
        )


def turn(couplings, transfers, top_turned, node_turned, leaf_turned):
    _, m, _, _ = place()
    for i in range(3):
        top_turned[i] = couplings[2, i].T
    node_turned[...] = transfers[1, m].T
    for i in range(4):
        leaf_turned[i] = transfers[0, i].T


def descend(c2, c3, c1, top_turned, node_turned, field, out):
    r = place()[0]
    g = sum(
        dot(c[...], top_turned[offset(r ^ d, r)], 1, 0) for d, c in zip((2, 3, 1), (c2, c3, c1))
    )
    out[...] = field[...] + dot(g, node_turned[...], 1, 0)


def relay(block, out):
    out[...] = block[...]


def finish(
    first, near_above, near_third, near_fourth, row_basis, leaf_turned, f0, g0, f1, g1, *rest
):
    out, block, whole, sems = rest[-4:]
    _, m, k, _ = place()
    wide, step = whole.shape[0], g0.shape[0]
    for j, (field, parent) in enumerate(((f0, g0), (f1, g1))):
        at = span((mine(m, k) ^ j) % 2, step)
        whole[at, :] = field[...] + dot(parent[...], leaf_turned[k], 1, 0)
    columns = span((mine(m, k) ^ first) // 2, wide)
    chunk = out.shape[0] // CHUNKS
    copies = []
    for i in range(CHUNKS):
        at = pl.ds(i * chunk, chunk)
        near = (near_above, near_above, near_third, near_fourth)[i]
        part = near[pl.ds(i * chunk % near.shape[0], chunk), columns]
        block[at, :] = part + dot(row_basis[at, :], whole[...], 1, 1)
        copy = pltpu.make_async_copy(block.at[at], out.at[at, columns], sems.at[i])
        copy.start()
        copies.append(copy)
    for copy in copies:
        copy.wait()


def far_block(near_above, near_third, near_fourth, row_basis, leaf_turned, field, parent, out):
    _, m, k, _ = place()
    columns = span(mine(m, k) ^ 2, out.shape[1])
    g = field[...] + dot(parent[...], leaf_turned[k], 1, 0)
    first_row = 0
    for near in (near_above, near_third, near_fourth):
        at = pl.ds(first_row, near.shape[0])
        out[at, :] = near[:, columns] + dot(row_basis[at, :], g, 1, 1)
        first_row += near.shape[0]


def finish_last(
    near_above, near_third, near_fourth, row_basis, leaf_turned, ready, field, parent, _, *rest
):
    out, block, sems = rest
    _, m, k, _ = place()
    wide = block.shape[1]
    copies = [pltpu.make_async_copy(ready, out.at[:, span(mine(m, k) ^ 2, wide)], sems.at[CHUNKS])]
    copies[0].start()
    g = field[...] + dot(parent[...], leaf_turned[k], 1, 0)
    columns = span(mine(m, k) ^ 3, wide)
    chunk = out.shape[0] // CHUNKS
    for i in range(CHUNKS):
        at = pl.ds(i * chunk, chunk)
        near = (near_above, near_above, near_third, near_fourth)[i]
        part = near[pl.ds(i * chunk % near.shape[0], chunk), columns]
        block[at, :] = part + dot(row_basis[at, :], g, 1, 1)
        copy = pltpu.make_async_copy(block.at[at], out.at[at, columns], sems.at[i])
        copy.start()
        copies.append(copy)
    for copy in copies:
        copy.wait()


def swap(block, bits):
    return lax.ppermute(block, "leaf", [(i, i ^ bits) for i in range(lax.axis_size("leaf"))])


def local(ratings, dense_blocks, row_basis, col_basis, transfers, couplings):
    users, columns = ratings.shape
    rank = col_basis.shape[2]
    quarter = columns // 4
    unit = 2 * 3 * rank * rank
    dense, rbasis, cbasis = dense_blocks[0], row_basis[0], col_basis[0]

    c2, c3, held, basis_held = pl.pallas_call(
        far_coefficients,
        out_shape=[
            pltpu.VMEM(shape, F32)
            for shape in ((quarter, rank), (quarter, rank), (users, columns), (users, rank))
        ],
        in_specs=[ANY] * 2,
        out_specs=[VMEM] * 4,
        scratch_shapes=[
            pltpu.VMEM((columns // 2, rank), F32),
            pltpu.SemaphoreType.DMA((2, CHUNKS)),
            pltpu.SemaphoreType.DMA,
        ],
        **settings(3 * users * columns * rank, users * columns, "far_coefficients"),
    )(*in_hbm([ratings, cbasis]))
    c2, c3 = swap(c2, 2), swap(c3, 3)
    half_rows = (users // 2, columns)
    dense_half = [pltpu.VMEM((users // 2, users), F32), pltpu.SemaphoreType.DMA((2,))]
    c0, c1, near_above = pl.pallas_call(
        own_and_near,
        out_shape=[pltpu.VMEM(shape, F32) for shape in ((quarter, rank), (quarter, rank), half_rows)],
        in_specs=[VMEM, VMEM, ANY],
        out_specs=[VMEM] * 3,
        scratch_shapes=[pltpu.VMEM((columns // 2, rank), F32), *dense_half],
        **settings(3 * users * users * columns, users * users, "own_and_near"),
    )(*in_vmem([held, basis_held]), *in_hbm([dense]))
    c1 = swap(c1, 1)
    leaves, coef = (0, 2, 3, 1), [c0, c2, c3, c1]
    (lifted,) = run(
        functools.partial(lift, 0, 2, leaves),
        [*coef, transfers],
        [(quarter, rank)],
        "lift_leaves",
        unit * columns,
    )
    nodes = (0, 1, 3, 2)
    node_coef = [swap(lifted, (j << 2) | (j & 2)) if j else lifted for j in nodes]
    part_rows = (users // 4, columns)
    near_third, dense_rest = pl.pallas_call(
        near_below,
        out_shape=[pltpu.VMEM(part_rows, F32), pltpu.VMEM((users // 4, users), F32)],
        in_specs=[ANY, VMEM, ANY],
        out_specs=[VMEM] * 2,
        scratch_shapes=[pltpu.VMEM((users // 4, users), F32), pltpu.SemaphoreType.DMA((3,))],
        **settings(users * users * columns, users * users, "near_below"),
    )(*in_hbm([dense]), *in_vmem([held]), lifted)
    leaf_fields = run(
        functools.partial(couple, 0, 2, leaves),
        [*coef, couplings],
        [(quarter, rank)] * 4,
        "couple_leaves",
        unit * 3 * columns,
    )
    turned = run(
        turn,
        [couplings, transfers],
        [(3, rank, rank), (rank, rank), (4, rank, rank)],
        "turn",
        unit * 8 * rank,
        after=[lifted],
    )
    (crown,) = run(
        functools.partial(lift, 1, 1, nodes),
        [*node_coef, transfers],
        [(quarter, rank)],
        "lift_nodes",
        unit * columns,
        after=[*leaf_fields, near_third, turned[1]],
    )
    top_coef = [swap(crown, bits) for bits in (32, 48, 16)]
    (node_field,) = run(
        functools.partial(couple, 1, 1, nodes),
        [*node_coef, couplings],
        [(quarter, rank)],
        "couple_nodes",
        unit * 3 * quarter,
    )
    fields = [leaf_fields[0]] + [swap(leaf_fields[j], j) for j in (1, 2, 3)]
    (parent,) = run(
        descend,
        [*top_coef, *turned[:2], node_field],
        [(quarter, rank)],
        "descend",
        unit * 4 * quarter,
        after=fields[2:3],
    )
    far_parent, core_parent = swap(parent, 2), swap(parent, 1)
    (near_fourth,) = run(
        near_last,
        [dense_rest, held],
        [part_rows],
        "near_last",
        3 * users * users * columns,
        after=[parent],
    )
    nears = [near_above, near_third, near_fourth]

    def write(first, pieces, out):
        ins = in_vmem([*nears, rbasis, turned[2], *pieces])
        return pl.pallas_call(
            functools.partial(finish, first),
            out_shape=pltpu.HBM((users, columns), F32),
            in_specs=[VMEM] * len(ins) + [ANY] * len(out),
            out_specs=ANY,
            scratch_shapes=[
                pltpu.VMEM((users, columns // 2), F32),
                pltpu.VMEM((columns // 2, rank), F32),
                pltpu.SemaphoreType.DMA((CHUNKS,)),
            ],
            input_output_aliases={len(ins): 0} if out else {},
            **settings(3 * users * rank * columns, users * columns, "finish_%d" % first),
        )(*ins, *out)

    out = write(0, [fields[0], parent, fields[1], core_parent], [])
    (far_parent,) = run(
        relay, [far_parent], [(quarter, rank)], "relay", quarter * rank, after=in_hbm([out])
    )
    (ready,) = run(
        far_block,
        [*nears, rbasis, turned[2], fields[2], far_parent],
        [(users, quarter)],
        "far_block",
        6 * users * rank * quarter,
    )
    ins = in_vmem([*nears, rbasis, turned[2], ready, fields[3], swap(far_parent, 1)])
    return pl.pallas_call(
        finish_last,
        out_shape=pltpu.HBM((users, columns), F32),
        in_specs=[VMEM] * len(ins) + [ANY],
        out_specs=ANY,
        scratch_shapes=[
            pltpu.VMEM((users, quarter), F32),
            pltpu.SemaphoreType.DMA((CHUNKS + 1,)),
        ],
        input_output_aliases={len(ins): 0},
        **settings(6 * users * rank * quarter, users * columns, "finish_last"),
    )(*ins, out)


def solution(mesh):
    placed = (
        P("leaf", "col"),
        P("leaf", None, None),
        P("leaf", None, None),
        P("leaf", None, None),
        P(),
        P(),
    )
    return jax.shard_map(
        local, mesh=mesh, in_specs=placed, out_specs=P("leaf", "col"), check_vma=False
    )
```
